256 devices in a mesh: rows: 128 (over y, z, x), rep: 2 (over core).
Axes of the slice: x: 4, y: 4, z: 8, core: 2. Of those that a mesh axis runs over, the one named last changes fastest.
Arguments:
- features: bfloat16 [131072, 128], P('rows'), may hold values from -6 to 6
- weight: bfloat16 [128, 256], replicated, may hold values from -0.5 to 0.5
- tiles: bfloat16 [1024, 64, 128, 128], P('rows', 'rep'), may hold values from -0.0625 to 0.0625
- tile_cols: int32 [1024, 64], P('rows', 'rep'), may hold values from 0 to 1023, as said below
- order: int32 [1024], replicated, may hold values from 0 to 1023, as said below
- cotangent: bfloat16 [131072, 256], P('rows'), may hold values from -24 to 24
Outputs:
- activated: bfloat16 [131072, 256], P('rows')
- feature_grad: float32 [131072, 128], P('rows')
- weight_grad: float32 [128, 256], replicated
The draws below stay inside these ranges and needn't reach their ends.
Inputs may be any that keep to these rules, and one draw needn't show every extreme that they name: `tile_cols`: the 64 column tiles of one tile row are all different. Among the 32 slots of the 8 tile rows that one index of rows and one index of rep hold, exactly 2 name (through order) blocks owned by each index of rows, that is blocks o * 8 to (o + 1) * 8 - 1 for index o; all blocks named by the slots of one index of rows are different. `order`: A permutation of the tile rows.
All inputs are finite; a program needn't handle non-finite values.
Results may differ from the reference program's by a relative error of at most 0.0055.
Values may be sent and summed in bfloat16 or wider, within the bound.
No kernel may reach another device: no remote copies, remote signals or barrier semaphores. Data moves between devices by JAX's collectives and lax.ppermute only.
A program may use at most 192 MiB of HBM per device.

```python
import jax
import jax.numpy as jnp
from jax import lax

FEAT = 128
HID = 256
TILE = 128
CAP = 2
TB = 8
KT_REP = 32
N_TILES = 1024
NODES = 131072
KT = 64


def shared_graph(key):
    n_rows = N_TILES // TB
    copies = KT // KT_REP
    slots = TB * KT_REP
    order = jax.random.permutation(jax.random.fold_in(key, 11), N_TILES).astype(jnp.int32)
    inverse = jnp.zeros((N_TILES,), jnp.int32).at[order].set(jnp.arange(N_TILES, dtype=jnp.int32))
    device_keys = jax.random.split(jax.random.fold_in(key, 12), n_rows * copies)
    places = jax.vmap(lambda k: jax.random.permutation(k, slots))(device_keys).astype(jnp.int32)
    places = places.reshape(n_rows, copies, slots)
    owner = places // CAP
    copy_index = places % CAP
    start_local = jax.random.randint(jax.random.fold_in(key, 13), (n_rows, n_rows), 0, TB).astype(jnp.int32)
    reader = jnp.arange(n_rows, dtype=jnp.int32)[:, None, None]
    core = jnp.arange(copies, dtype=jnp.int32)[None, :, None]
    base = start_local[reader, owner]
    local = (base + copy_index * copies + core) % TB
    block = owner * TB + local
    cols = inverse[block]
    cols = cols.reshape(n_rows, copies, TB, KT_REP).transpose(0, 2, 1, 3).reshape(N_TILES, KT)
    return (order, cols.astype(jnp.int32))


def draw_order(key, part):
    return shared_graph(key)[0]


def draw_tile_cols(key, part):
    return shared_graph(key)[1]


def raised(entries, rng, source, target, parts, factor):
    def block_of(position):
        return (jnp.arange(entries.shape[position]) // (entries.shape[position] // parts)).reshape((-1,) + (1,) * (entries.ndim - 1 - position))

    first = jax.random.permutation(rng, parts)[block_of(target)]
    second = (block_of(target) + parts // 2) % parts
    return jnp.where((block_of(source) == first) | (block_of(source) == second), factor * entries, entries)


def block_scale(key, shape, cuts, low, largest):
    gain = 1.0
    for position, shards_of in cuts:
        steps = jax.random.uniform(jax.random.fold_in(jax.random.fold_in(key, 6), position), (shards_of,), jnp.float32, low / len(cuts), largest / len(cuts))
        gain = gain * jnp.repeat(jnp.exp(steps), shape[position] // shards_of).reshape((-1,) + (1,) * (len(shape) - 1 - position))
    return gain


def noise(stream_key, dims, scale, limit, cuts=(), kind=jnp.bfloat16):
    values = jax.random.normal(stream_key, dims, jnp.float32) * scale
    if len(cuts) > 0:
        values = block_scale(stream_key, dims, cuts, -0.22, 0.18) * values
    return jnp.clip(values, min=-limit, max=limit).astype(kind)


def bell_draw_with(rng, extent, scale, most, cuts, heavy, kind=jnp.bfloat16):
    drawn = scale * jax.random.normal(rng, extent, jnp.float32)
    if cuts:
        drawn = drawn * block_scale(rng, extent, cuts, -0.22, 0.18)
    return jnp.clip(raised(drawn, jax.random.fold_in(rng, 3), *heavy), -most, most).astype(kind)


def setup_inputs(seed: int = 0) -> dict:
    seeds = jax.random.split(jax.random.key(seed), 7)
    features = noise(seeds[0], (NODES, FEAT), 1.0, 6.0, ((0, 128),))
    weight = noise(seeds[1], (FEAT, HID), FEAT ** -0.5, 0.5)
    tiles = noise(seeds[2], (N_TILES, KT, TILE, TILE), (KT * TILE) ** -0.5, 0.0625, ((0, 128), (1, 2)))
    tile_cols = draw_tile_cols(jax.random.fold_in(seeds[6], 71), 0)
    order = draw_order(jax.random.fold_in(seeds[6], 71), 0)
    cotangent = bell_draw_with(seeds[5], (NODES, HID), 1.0, 24.0, ((0, 128),), (0, 1, 128, 5.5))
    return {"features": features, "weight": weight, "tiles": tiles, "tile_cols": tile_cols, "order": order, "cotangent": cotangent}


def reference(features, weight, tiles, tile_cols, order, cotangent):
    n_tiles = tile_cols.shape[0]
    side = tiles.shape[2]
    width = features.shape[1]
    feature_blocks = features.reshape(n_tiles, side, width)
    block = order[tile_cols].astype(jnp.int32)

    def forward_row(pair):
        row_tiles, row_block = pair
        picked = feature_blocks[row_block]
        return jnp.einsum("kij,kjf->if", row_tiles.astype(jnp.float32), picked.astype(jnp.float32))

    summed = lax.map(forward_row, (tiles, block)).reshape(-1, width)
    aggregated = summed.astype(jnp.bfloat16)
    pre = jnp.dot(aggregated, weight, preferred_element_type=jnp.float32)
    sig = jax.nn.sigmoid(pre)
    activated = (pre * sig).astype(jnp.bfloat16)
    pre_grad = (cotangent.astype(jnp.float32) * sig * (1.0 + pre * (1.0 - sig))).astype(jnp.bfloat16)
    weight_grad = jnp.dot(aggregated.T, pre_grad, preferred_element_type=jnp.float32)
    spread = jnp.dot(pre_grad, weight.T, preferred_element_type=jnp.float32).astype(jnp.bfloat16)
    spread_blocks = spread.reshape(n_tiles, side, width)

    def backward_row(total, triple):
        row_tiles, row_block, row_spread = triple
        terms = jnp.einsum("kij,if->kjf", row_tiles.astype(jnp.float32), row_spread.astype(jnp.float32))
        return total.at[row_block].add(terms), None

    start = jnp.zeros((n_tiles, side, width), jnp.float32)
    feature_grad, unused = lax.scan(backward_row, start, (tiles, block, spread_blocks))
    return activated, feature_grad.reshape(-1, width), weight_grad
```

```python
import functools

import jax
import jax.numpy as jnp
from jax import lax
from jax.experimental import pallas as pl
from jax.experimental.pallas import tpu as pltpu
from jax.sharding import PartitionSpec as P

BF = jnp.bfloat16
F32 = jnp.float32
BOTH = ("rows", "rep")
SWAP = ((0, 1), (1, 0))


def torus(n_rows):
    return {128: (4, 8, 4), 8: (2, 2, 2)}[n_rows]


def ring(n_rows, axis):
    sizes = torus(n_rows)
    pairs = []
    for i in range(n_rows):
        c = [i // (sizes[1] * sizes[2]), i // sizes[2] % sizes[1], i % sizes[2]]
        for core in range(2):
            t = list(c)
            t[axis] = (t[axis] + (1 if core == 0 else -1)) % sizes[axis]
            pairs.append((2 * i + core, 2 * ((t[0] * sizes[1] + t[1]) * sizes[2] + t[2]) + core))
    return tuple(pairs)


PARTS = ((0, 2, (2, 0, 1)), (2, 3, (0, 1, 2)), (5, 3, (1, 2, 0)))


def gather_parts(n_rows, own):
    sizes = torus(n_rows)
    out = []
    for first, count, axes in PARTS:
        held = own[first : first + count]
        for axis in axes:
            pieces = [held]
            for _ in range(sizes[axis] - 1):
                pieces.append(lax.ppermute(pieces[-1], BOTH, ring(n_rows, axis)))
            if axis == axes[-1]:
                out.extend(pieces)
            else:
                held = jnp.concatenate(pieces, 0)
    return jnp.concatenate(out, 0)


def scatter_parts(n_rows, terms):
    sizes = torus(n_rows)
    out = []
    for first, count, axes in PARTS:
        held = terms[first * n_rows : (first + count) * n_rows]
        for axis in axes[::-1]:
            n = sizes[axis]
            size = held.shape[0] // n
            total = held[(n - 1) * size :]
            for d in range(n - 2, -1, -1):
                came = lax.ppermute(total, BOTH, ring(n_rows, axis))
                total = came.astype(F32) + held[d * size : (d + 1) * size].astype(F32)
                if d > 0 or axis != axes[0]:
                    total = total.astype(BF)
            held = total
        out.append(held)
    return jnp.concatenate(out, 0)


def positions(n_rows, tile_rows, block, here, core, sign):
    sizes = torus(n_rows)
    owner, local = block // tile_rows, block % tile_rows

    def split(i):
        return (i // (sizes[1] * sizes[2]), i // sizes[2] % sizes[1], i % sizes[2])

    turn = jnp.where(core == 0, sign, -sign)
    mine, theirs = split(here), split(owner)
    offset = [(turn * (mine[a] - theirs[a]) + sizes[a]) % sizes[a] for a in range(3)]
    place = jnp.zeros_like(block)
    for first, count, axes in PARTS:
        a, b, c = axes
        at = ((offset[c] * sizes[b] + offset[b]) * sizes[a] + offset[a]) * count + local - first
        place = jnp.where((local >= first) & (local < first + count), first * n_rows + at, place)
    return place


def pack_kernel(width, core_ref, tiles_ref, own_ref, send_ref, zero_ref):
    side = tiles_ref.shape[2]
    half = side // 2
    zero_ref[...] = jnp.zeros_like(zero_ref)

    def fill(first, second):
        for q in range(tiles_ref.shape[1] // width):
            group = [tiles_ref[0, q * width + i] for i in range(width)]
            first[0, q] = jnp.concatenate([t[:, :half] for t in group], 1)
            second[0, q] = jnp.concatenate([t[:, half:] for t in group], 1)

    @pl.when(core_ref[0] == 0)
    def _():
        fill(own_ref, send_ref)

    @pl.when(core_ref[0] != 0)
    def _():
        fill(send_ref, own_ref)


def pack(core, tiles, n_tiles, width):
    rows, slots, side, _ = tiles.shape
    packed = jax.ShapeDtypeStruct((rows, slots // width, side, width * side // 2), BF)
    spec = pl.BlockSpec((1, slots // width, side, width * side // 2), lambda b: (b, 0, 0, 0))
    zeros = jax.ShapeDtypeStruct((n_tiles, side // 2, side), BF)
    return pl.pallas_call(
        functools.partial(pack_kernel, width),
        grid=(rows,),
        in_specs=[
            pl.BlockSpec(memory_space=pltpu.SMEM),
            pl.BlockSpec((1, slots, side, side), lambda b: (b, 0, 0, 0)),
        ],
        out_specs=[
            spec,
            spec,
            pl.BlockSpec((n_tiles // rows, side // 2, side), lambda b: (b, 0, 0)),
        ],
        out_shape=[packed, packed, zeros],
        compiler_params=pltpu.CompilerParams(vmem_limit_bytes=40 * 2**20),
        cost_estimate=pl.CostEstimate(flops=0, bytes_accessed=33 * 2**20, transcendentals=0),
        name="pack_tiles",
    )(core, tiles)


def forward_kernel(place_ref, own_ref, other_ref, blocks_ref, sum_ref, held, sems):
    b = pl.program_id(0)
    rows = pl.num_programs(0)
    slots = held.shape[1]
    half = held.shape[2]

    def fetch(row):
        slot = lax.rem(row, 2)

        @pl.loop(0, slots, unroll=8)
        def _(k):
            at = place_ref[row * slots + k]
            pltpu.make_async_copy(blocks_ref.at[at], held.at[slot, k], sems.at[slot]).start()

    @pl.when(b == 0)
    def _():
        fetch(b)

    @pl.when(b + 1 < rows)
    def _():
        fetch(b + 1)

    now = lax.rem(b, 2)
    pltpu.make_async_copy(blocks_ref.at[pl.ds(0, slots)], held.at[now], sems.at[now]).wait()
    total = jnp.zeros(sum_ref.shape[1:], F32)
    width = own_ref.shape[3] // half
    k = 0
    for ref in (own_ref, other_ref):
        for q in range(ref.shape[1]):
            right = held[now, k : k + width].reshape(width * half, -1)
            total += jnp.dot(ref[0, q], right, preferred_element_type=F32)
            k += width
    sum_ref[0] = total


def forward(place, own, other, blocks):
    rows, groups, side, wide = own.shape
    slots = place.shape[0] // rows
    spec = pl.BlockSpec((1, groups, side, wide), lambda b: (b, 0, 0, 0))
    return pl.pallas_call(
        forward_kernel,
        grid=(rows,),
        in_specs=[
            pl.BlockSpec(memory_space=pltpu.SMEM),
            spec,
            spec,
            pl.BlockSpec(memory_space=pl.ANY),
        ],
        out_specs=pl.BlockSpec((1, side, blocks.shape[2]), lambda b: (b, 0, 0)),
        out_shape=jax.ShapeDtypeStruct((rows, side, blocks.shape[2]), F32),
        scratch_shapes=[
            pltpu.VMEM((2, slots) + blocks.shape[1:], BF),
            pltpu.SemaphoreType.DMA((2,)),
        ],
        compiler_params=pltpu.CompilerParams(vmem_limit_bytes=40 * 2**20),
        cost_estimate=pl.CostEstimate(flops=2**30, bytes_accessed=2**24, transcendentals=0),
        name="forward_tiles",
    )(place, own, other, blocks)


def backward_kernel(
    core_ref, place_ref, mine_ref, came_ref, weight_ref, cot_ref, own_ref, other_ref, zero_ref,
    act_ref, terms_ref, wgrad_ref, held, sems,
):
    b = pl.program_id(0)
    rows = pl.num_programs(0)
    slots = held.shape[1]
    half = held.shape[2]
    now = lax.rem(b, 2)

    def drain(slot):
        pltpu.make_async_copy(held.at[slot], terms_ref.at[pl.ds(0, slots)], sems.at[slot]).wait()

    agg = (mine_ref[0] + came_ref[0]).astype(BF)
    weight = weight_ref[...]
    pre = jnp.dot(agg, weight, preferred_element_type=F32)
    sig = jax.nn.sigmoid(pre)
    act_ref[0] = (pre * sig).astype(BF)
    grad = (cot_ref[0].astype(F32) * sig * (1.0 + pre * (1.0 - sig))).astype(BF)
    spread = lax.dot_general(
        grad, weight, (((1,), (1,)), ((), ())), preferred_element_type=F32
    ).astype(BF)
    hid = grad.shape[1] // 2
    part = jnp.where(core_ref[0] == 0, grad[:, :hid].astype(F32), grad[:, hid:].astype(F32)).astype(BF)
    wgrad = lax.dot_general(agg, part, (((0,), (0,)), ((), ())), preferred_element_type=F32)

    @pl.when(b == 0)
    def _():
        wgrad_ref[...] = wgrad

    @pl.when(b > 0)
    def _():
        wgrad_ref[...] += wgrad

    @pl.when(b >= 2)
    def _():
        drain(now)

    width = own_ref.shape[3] // half
    k = 0
    for ref in (own_ref, other_ref):
        for q in range(ref.shape[1]):
            term = lax.dot_general(
                ref[0, q], spread, (((0,), (0,)), ((), ())), preferred_element_type=F32
            ).astype(BF)
            held[now, k : k + width] = term.reshape(width, half, -1)
            k += width

    @pl.loop(0, slots, unroll=8)
    def _(k):
        at = place_ref[b * slots + k]
        pltpu.make_async_copy(held.at[now, k], terms_ref.at[at], sems.at[now]).start()

    @pl.when(b == rows - 1)
    def _():
        drain(lax.rem(b + 1, 2))
        drain(now)


def backward(core, place, mine, came, weight, cotangent, own, other, zeros):
    rows, groups, side, wide = own.shape
    slots = place.shape[0] // rows
    feat, hid = weight.shape
    tile_spec = pl.BlockSpec((1, groups, side, wide), lambda b: (b, 0, 0, 0))
    row_spec = pl.BlockSpec((1, side, feat), lambda b: (b, 0, 0))
    hid_spec = pl.BlockSpec((1, side, hid), lambda b: (b, 0, 0))
    smem = pl.BlockSpec(memory_space=pltpu.SMEM)
    return pl.pallas_call(
        backward_kernel,
        grid=(rows,),
        in_specs=[
            smem,
            smem,
            row_spec,
            row_spec,
            pl.BlockSpec((feat, hid), lambda b: (0, 0)),
            hid_spec,
            tile_spec,
            tile_spec,
            pl.BlockSpec(memory_space=pl.ANY),
        ],
        out_specs=[
            hid_spec,
            pl.BlockSpec(memory_space=pl.ANY),
            pl.BlockSpec((feat, hid // 2), lambda b: (0, 0)),
        ],
        out_shape=[
            jax.ShapeDtypeStruct((rows, side, hid), BF),
            jax.ShapeDtypeStruct(zeros.shape, BF),
            jax.ShapeDtypeStruct((feat, hid // 2), F32),
        ],
        scratch_shapes=[
            pltpu.VMEM((2, slots) + zeros.shape[1:], BF),
            pltpu.SemaphoreType.DMA((2,)),
        ],
        input_output_aliases={8: 1},
        compiler_params=pltpu.CompilerParams(vmem_limit_bytes=40 * 2**20),
        cost_estimate=pl.CostEstimate(flops=2**30, bytes_accessed=2**24, transcendentals=2**18),
        name="backward_tiles",
    )(core, place, mine, came, weight, cotangent, own, other, zeros)


def body(features, weight, tiles, tile_cols, order, cotangent):
    tile_rows, row_slots, side, _ = tiles.shape
    width = features.shape[1]
    n_tiles = order.shape[0]
    n_rows = lax.axis_size("rows")
    here = lax.axis_index("rows")
    core = lax.axis_index("rep")
    core_ref = core.reshape(1).astype(jnp.int32)
    half = side // 2
    group = 4 if row_slots % 4 == 0 else 2

    halves = features.reshape(tile_rows, 2, half, width)
    own_half = jnp.where(core == 0, halves[:, 0], halves[:, 1])
    gathered = gather_parts(n_rows, own_half)

    own, send, zeros = pack(core_ref, tiles, n_tiles, group)
    other = lax.ppermute(send, "rep", SWAP)

    labels = jnp.arange(n_tiles, dtype=jnp.int32)
    flat = tile_cols.reshape(-1)
    block = jnp.sum(jnp.where(flat[:, None] == labels[None, :], order[None, :], 0), axis=1)
    block = block.reshape(tile_rows, row_slots)
    block = jnp.concatenate([block, lax.ppermute(block, "rep", SWAP)], 1).reshape(-1)
    gather_place = positions(n_rows, tile_rows, block, here, core, 1)
    scatter_place = positions(n_rows, tile_rows, block, here, core, -1)

    mine = forward(gather_place, own, other, gathered)
    came = lax.ppermute(mine, "rep", SWAP)
    activated, terms, wgrad = backward(
        core_ref, scatter_place, mine, came, weight,
        cotangent.reshape(tile_rows, side, -1), own, other, zeros,
    )

    bit = 1
    while bit < n_rows:
        wgrad = wgrad + lax.ppermute(wgrad, "rows", tuple((i, i ^ bit) for i in range(n_rows)))
        bit *= 2
    wother = lax.ppermute(wgrad, "rep", SWAP)
    weight_grad = jnp.where(
        core == 0, jnp.concatenate([wgrad, wother], 1), jnp.concatenate([wother, wgrad], 1)
    )

    owned = scatter_parts(n_rows, terms)
    pair = lax.ppermute(owned, "rep", SWAP)
    feature_grad = jnp.where(
        core == 0, jnp.stack([owned, pair], 1), jnp.stack([pair, owned], 1)
    ).reshape(tile_rows * side, width)
    return activated.reshape(tile_rows * side, -1), feature_grad, weight_grad


def solution(mesh):
    in_specs = (
        P("rows", None),
        P(),
        P("rows", "rep", None, None),
        P("rows", "rep"),
        P(),
        P("rows", None),
    )
    out_specs = (P("rows", None), P("rows", None), P())
    return jax.shard_map(body, mesh=mesh, in_specs=in_specs, out_specs=out_specs, check_vma=False)
```

```python
import functools

import jax
import jax.numpy as jnp
from jax import lax
from jax.experimental import pallas as pl
from jax.experimental.pallas import tpu as pltpu
from jax.sharding import PartitionSpec as P

BF = jnp.bfloat16
F32 = jnp.float32
BOTH = ("rows", "rep")
SWAP = ((0, 1), (1, 0))


def torus(n_rows):
    return {128: (4, 8, 4), 8: (2, 2, 2)}[n_rows]


def swap(n_rows, axis, turn):
    sizes = torus(n_rows)
    pairs = []
    for i in range(n_rows):
        c = [i // (sizes[1] * sizes[2]), i // sizes[2] % sizes[1], i % sizes[2]]
        for core in range(2):
            t = list(c)
            t[axis] = (t[axis] + (1 if (t[axis] + core + turn) % 2 == 0 else -1)) % sizes[axis]
            pairs.append((2 * i + core, 2 * ((t[0] * sizes[1] + t[1]) * sizes[2] + t[2]) + core))
    return tuple(pairs)


PARTS = ((0, 2, (2, 0, 1)), (2, 3, (0, 1, 2)), (5, 3, (1, 2, 0)))
ARRIVAL = {2: (0, 1), 4: (0, 1, 3, 2), 8: (0, 1, 7, 6, 2, 3, 5, 4)}


def gather_chain(n_rows, own, axes):
    sizes = torus(n_rows)
    held = own
    for axis in axes:
        pieces = [held]
        send = held
        for step in range(sizes[axis] // 2):
            got = yield send, BOTH, swap(n_rows, axis, step % 2)
            pieces.append(got)
            send = jnp.concatenate([held, got], 0) if step == 0 else got
        if axis == axes[-1]:
            return pieces
        held = jnp.concatenate(pieces, 0)


def scatter_chain(n_rows, held, axes):
    sizes = torus(n_rows)
    for axis in axes[::-1]:
        n = sizes[axis]
        size = held.shape[0] // n
        total = held[(n - 2) * size :]
        for step in range(n // 2 - 1, 0, -1):
            got = yield total, BOTH, swap(n_rows, axis, step % 2)
            kept = held[(2 * step - 2) * size : 2 * step * size]
            total = (got.astype(F32) + kept.astype(F32)).astype(BF)
        got = yield total[size:], BOTH, swap(n_rows, axis, 0)
        held = total[:size].astype(F32) + got.astype(F32)
        if axis != axes[0]:
            held = held.astype(BF)
    return held


def sum_chain(n_rows, part):
    bit = 1
    while bit < n_rows:
        part = part + (yield part, "rows", tuple((i, i ^ bit) for i in range(n_rows)))
        bit *= 2
    return part, (yield part, "rep", SWAP)


def drive(chains, plan):
    asks = [next(c) for c in chains]
    flying = {}
    results = [None] * len(chains)

    def finish(names):
        names = [i for i in names if i in flying]
        if not names:
            return
        values = lax.optimization_barrier(tuple(flying.pop(i) for i in names))
        for i, value in zip(names, values):
            try:
                asks[i] = chains[i].send(value)
            except StopIteration as stop:
                asks[i], results[i] = None, stop.value

    def start(names):
        for i in names:
            if asks[i] is not None and i not in flying:
                flying[i] = lax.ppermute(*asks[i])

    for starts, ends in plan:
        start(starts)
        finish(ends)
    every = range(len(chains))
    while any(ask is not None for ask in asks):
        start(every)
        finish(every)
    return results


def positions(n_rows, tile_rows, block, here, core):
    sizes = torus(n_rows)
    owner, local = block // tile_rows, block % tile_rows

    def split(i):
        return (i // (sizes[1] * sizes[2]), i // sizes[2] % sizes[1], i % sizes[2])

    mine, theirs = split(here), split(owner)
    slot = []
    for axis in range(3):
        n = sizes[axis]
        turn = jnp.where((mine[axis] + core) % 2 == 0, 1, -1)
        offset = (turn * (theirs[axis] - mine[axis]) + n) % n
        slot.append(sum(jnp.where(offset == e, i, 0) for i, e in enumerate(ARRIVAL[n])))
    place = jnp.zeros_like(block)
    for first, count, axes in PARTS:
        a, b, c = axes
        at = ((slot[c] * sizes[b] + slot[b]) * sizes[a] + slot[a]) * count + local - first
        place = jnp.where((local >= first) & (local < first + count), first * n_rows + at, place)
    return place


def pack_kernel(width, core_ref, tiles_ref, own_ref, send_ref, zero_ref):
    side = tiles_ref.shape[2]
    half = side // 2
    zero_ref[...] = jnp.zeros_like(zero_ref)

    def fill(first, second):
        for q in range(tiles_ref.shape[1] // width):
            group = [tiles_ref[0, q * width + i] for i in range(width)]
            first[0, q] = jnp.concatenate([t[:, :half] for t in group], 1)
            second[0, q] = jnp.concatenate([t[:, half:] for t in group], 1)

    @pl.when(core_ref[0] == 0)
    def _():
        fill(own_ref, send_ref)

    @pl.when(core_ref[0] != 0)
    def _():
        fill(send_ref, own_ref)


def pack(core, tiles, n_tiles, width):
    rows, slots, side, _ = tiles.shape
    packed = jax.ShapeDtypeStruct((rows, slots // width, side, width * side // 2), BF)
    spec = pl.BlockSpec((1, slots // width, side, width * side // 2), lambda b: (b, 0, 0, 0))
    zeros = jax.ShapeDtypeStruct((n_tiles, side // 2, side), BF)
    return pl.pallas_call(
        functools.partial(pack_kernel, width),
        grid=(rows,),
        in_specs=[
            pl.BlockSpec(memory_space=pltpu.SMEM),
            pl.BlockSpec((1, slots, side, side), lambda b: (b, 0, 0, 0)),
        ],
        out_specs=[
            spec,
            spec,
            pl.BlockSpec((n_tiles // rows, side // 2, side), lambda b: (b, 0, 0)),
        ],
        out_shape=[packed, packed, zeros],
        compiler_params=pltpu.CompilerParams(vmem_limit_bytes=40 * 2**20),
        cost_estimate=pl.CostEstimate(flops=0, bytes_accessed=33 * 2**20, transcendentals=0),
        name="pack_tiles",
    )(core, tiles)


def forward_kernel(place_ref, own_ref, other_ref, blocks_ref, sum_ref, held, sems):
    b = pl.program_id(0)
    rows = pl.num_programs(0)
    slots = held.shape[1]
    half = held.shape[2]

    def fetch(row):
        slot = lax.rem(row, 2)

        @pl.loop(0, slots, unroll=8)
        def _(k):
            at = place_ref[row * slots + k]
            pltpu.make_async_copy(blocks_ref.at[at], held.at[slot, k], sems.at[slot]).start()

    @pl.when(b == 0)
    def _():
        fetch(b)

    @pl.when(b + 1 < rows)
    def _():
        fetch(b + 1)

    now = lax.rem(b, 2)
    pltpu.make_async_copy(blocks_ref.at[pl.ds(0, slots)], held.at[now], sems.at[now]).wait()
    total = jnp.zeros(sum_ref.shape[1:], F32)
    width = own_ref.shape[3] // half
    k = 0
    for ref in (own_ref, other_ref):
        for q in range(ref.shape[1]):
            right = held[now, k : k + width].reshape(width * half, -1)
            total += jnp.dot(ref[0, q], right, preferred_element_type=F32)
            k += width
    sum_ref[0] = total


def forward(place, own, other, blocks):
    rows, groups, side, wide = own.shape
    slots = place.shape[0] // rows
    spec = pl.BlockSpec((1, groups, side, wide), lambda b: (b, 0, 0, 0))
    return pl.pallas_call(
        forward_kernel,
        grid=(rows,),
        in_specs=[
            pl.BlockSpec(memory_space=pltpu.SMEM),
            spec,
            spec,
            pl.BlockSpec(memory_space=pl.ANY),
        ],
        out_specs=pl.BlockSpec((1, side, blocks.shape[2]), lambda b: (b, 0, 0)),
        out_shape=jax.ShapeDtypeStruct((rows, side, blocks.shape[2]), F32),
        scratch_shapes=[
            pltpu.VMEM((2, slots) + blocks.shape[1:], BF),
            pltpu.SemaphoreType.DMA((2,)),
        ],
        compiler_params=pltpu.CompilerParams(vmem_limit_bytes=40 * 2**20),
        cost_estimate=pl.CostEstimate(flops=2**30, bytes_accessed=2**24, transcendentals=0),
        name="forward_tiles",
    )(place, own, other, blocks)


def backward_kernel(
    core_ref, place_ref, mine_ref, came_ref, weight_ref, cot_ref, own_ref, other_ref, zero_ref,
    act_ref, terms_ref, wgrad_ref, held, sems,
):
    b = pl.program_id(0)
    rows = pl.num_programs(0)
    slots = held.shape[1]
    half = held.shape[2]
    now = lax.rem(b, 2)

    def drain(slot):
        pltpu.make_async_copy(held.at[slot], terms_ref.at[pl.ds(0, slots)], sems.at[slot]).wait()

    agg = (mine_ref[0] + came_ref[0]).astype(BF)
    weight = weight_ref[...]
    pre = jnp.dot(agg, weight, preferred_element_type=F32)
    sig = jax.nn.sigmoid(pre)
    act_ref[0] = (pre * sig).astype(BF)
    grad = (cot_ref[0].astype(F32) * sig * (1.0 + pre * (1.0 - sig))).astype(BF)
    spread = lax.dot_general(
        grad, weight, (((1,), (1,)), ((), ())), preferred_element_type=F32
    ).astype(BF)
    hid = grad.shape[1] // 2
    part = jnp.where(core_ref[0] == 0, grad[:, :hid].astype(F32), grad[:, hid:].astype(F32)).astype(BF)
    wgrad = lax.dot_general(agg, part, (((0,), (0,)), ((), ())), preferred_element_type=F32)

    @pl.when(b == 0)
    def _():
        wgrad_ref[...] = wgrad

    @pl.when(b > 0)
    def _():
        wgrad_ref[...] += wgrad

    @pl.when(b >= 2)
    def _():
        drain(now)

    width = own_ref.shape[3] // half
    k = 0
    for ref in (own_ref, other_ref):
        for q in range(ref.shape[1]):
            term = lax.dot_general(
                ref[0, q], spread, (((0,), (0,)), ((), ())), preferred_element_type=F32
            ).astype(BF)
            held[now, k : k + width] = term.reshape(width, half, -1)
            k += width

    @pl.loop(0, slots, unroll=8)
    def _(k):
        at = place_ref[b * slots + k]
        pltpu.make_async_copy(held.at[now, k], terms_ref.at[at], sems.at[now]).start()

    @pl.when(b == rows - 1)
    def _():
        drain(lax.rem(b + 1, 2))
        drain(now)


def backward(core, place, mine, came, weight, cotangent, own, other, zeros):
    rows, groups, side, wide = own.shape
    slots = place.shape[0] // rows
    feat, hid = weight.shape
    tile_spec = pl.BlockSpec((1, groups, side, wide), lambda b: (b, 0, 0, 0))
    row_spec = pl.BlockSpec((1, side, feat), lambda b: (b, 0, 0))
    hid_spec = pl.BlockSpec((1, side, hid), lambda b: (b, 0, 0))
    smem = pl.BlockSpec(memory_space=pltpu.SMEM)
    return pl.pallas_call(
        backward_kernel,
        grid=(rows,),
        in_specs=[
            smem,
            smem,
            row_spec,
            row_spec,
            pl.BlockSpec((feat, hid), lambda b: (0, 0)),
            hid_spec,
            tile_spec,
            tile_spec,
            pl.BlockSpec(memory_space=pl.ANY),
        ],
        out_specs=[
            hid_spec,
            pl.BlockSpec(memory_space=pl.ANY),
            pl.BlockSpec((feat, hid // 2), lambda b: (0, 0)),
        ],
        out_shape=[
            jax.ShapeDtypeStruct((rows, side, hid), BF),
            jax.ShapeDtypeStruct(zeros.shape, BF),
            jax.ShapeDtypeStruct((feat, hid // 2), F32),
        ],
        scratch_shapes=[
            pltpu.VMEM((2, slots) + zeros.shape[1:], BF),
            pltpu.SemaphoreType.DMA((2,)),
        ],
        input_output_aliases={8: 1},
        compiler_params=pltpu.CompilerParams(vmem_limit_bytes=40 * 2**20),
        cost_estimate=pl.CostEstimate(flops=2**30, bytes_accessed=2**24, transcendentals=2**18),
        name="backward_tiles",
    )(core, place, mine, came, weight, cotangent, own, other, zeros)


def body(features, weight, tiles, tile_cols, order, cotangent):
    tile_rows, row_slots, side, _ = tiles.shape
    width = features.shape[1]
    n_tiles = order.shape[0]
    n_rows = lax.axis_size("rows")
    here = lax.axis_index("rows")
    core = lax.axis_index("rep")
    core_ref = core.reshape(1).astype(jnp.int32)
    half = side // 2
    group = 4 if row_slots % 4 == 0 else 2

    halves = features.reshape(tile_rows, 2, half, width)
    own_half = jnp.where(core == 0, halves[:, 0], halves[:, 1])
    every = (0, 1, 2)
    late = ((every, every),) * 4 + (((1, 2, 0), (1, 2)), ((1, 2), every), (every, every))
    pieces = drive(
        [gather_chain(n_rows, own_half[f : f + c], axes) for f, c, axes in PARTS],
        late if n_rows == 128 else (),
    )
    gathered = jnp.concatenate([p for part in pieces for p in part], 0)

    own, send, zeros = pack(core_ref, tiles, n_tiles, group)
    other = lax.ppermute(send, "rep", SWAP)

    labels = jnp.arange(n_tiles, dtype=jnp.int32)
    flat = tile_cols.reshape(-1)
    block = jnp.sum(jnp.where(flat[:, None] == labels[None, :], order[None, :], 0), axis=1)
    block = block.reshape(tile_rows, row_slots)
    block = jnp.concatenate([block, lax.ppermute(block, "rep", SWAP)], 1).reshape(-1)
    place = positions(n_rows, tile_rows, block, here, core)

    mine = forward(place, own, other, gathered)
    came = lax.ppermute(mine, "rep", SWAP)
    activated, terms, wgrad = backward(
        core_ref, place, mine, came, weight,
        cotangent.reshape(tile_rows, side, -1), own, other, zeros,
    )

    every = (0, 1, 2, 3)
    early = (
        ((0, 1, 2, 3), (0, 3)),
        ((0, 3), (0, 1, 2, 3)),
        (every, every),
        ((0, 1, 2, 3), (1, 2, 3)),
        ((1, 2, 3), every),
    )
    chains = [
        scatter_chain(n_rows, terms[f * n_rows : (f + c) * n_rows], axes) for f, c, axes in PARTS
    ]
    *owned, (wgrad, wother) = drive(
        chains + [sum_chain(n_rows, wgrad)], early if n_rows == 128 else ()
    )
    weight_grad = jnp.where(
        core == 0, jnp.concatenate([wgrad, wother], 1), jnp.concatenate([wother, wgrad], 1)
    )
    owned = jnp.concatenate(owned, 0)
    pair = lax.ppermute(owned, "rep", SWAP)
    feature_grad = jnp.where(
        core == 0, jnp.stack([owned, pair], 1), jnp.stack([pair, owned], 1)
    ).reshape(tile_rows * side, width)
    return activated.reshape(tile_rows * side, -1), feature_grad, weight_grad


def solution(mesh):
    in_specs = (
        P("rows", None),
        P(),
        P("rows", "rep", None, None),
        P("rows", "rep"),
        P(),
        P("rows", None),
    )
    out_specs = (P("rows", None), P("rows", None), P())
    return jax.shard_map(body, mesh=mesh, in_specs=in_specs, out_specs=out_specs, check_vma=False)
```

```python
import functools

import jax
import jax.numpy as jnp
from jax import lax
from jax.experimental import pallas as pl
from jax.experimental.pallas import tpu as pltpu
from jax.sharding import PartitionSpec as P

BF = jnp.bfloat16
F32 = jnp.float32
BOTH = ("rows", "rep")
SWAP = ((0, 1), (1, 0))


def torus(n_rows):
    return {128: (4, 8, 4), 8: (2, 2, 2)}[n_rows]


def swap(n_rows, axis, turn):
    sizes = torus(n_rows)
    pairs = []
    for i in range(n_rows):
        c = [i // (sizes[1] * sizes[2]), i // sizes[2] % sizes[1], i % sizes[2]]
        for core in range(2):
            t = list(c)
            t[axis] = (t[axis] + (1 if (t[axis] + core + turn) % 2 == 0 else -1)) % sizes[axis]
            pairs.append((2 * i + core, 2 * ((t[0] * sizes[1] + t[1]) * sizes[2] + t[2]) + core))
    return tuple(pairs)


PARTS = ((0, 2, (2, 0, 1)), (2, 3, (0, 1, 2)), (5, 3, (1, 2, 0)))
ARRIVAL = {2: (0, 1), 4: (0, 1, 3, 2), 8: (0, 1, 7, 6, 2, 3, 5, 4)}


def gather_chain(n_rows, own, axes):
    sizes = torus(n_rows)
    held = own
    for axis in axes:
        n = sizes[axis]
        ahead, back = swap(n_rows, axis, 0), swap(n_rows, axis, 1)
        if axis == axes[-1] and n == 4:
            one, two = yield [(held, BOTH, ahead), (held, BOTH, back)]
            (far,) = yield [(one, BOTH, back)]
            return [held, one, two, far]
        pieces = [held]
        send = held
        for step in range(n // 2):
            (got,) = yield [(send, BOTH, back if step % 2 else ahead)]
            pieces.append(got)
            send = jnp.concatenate([held, got], 0) if step == 0 else got
        if axis == axes[-1]:
            return pieces
        held = lax.optimization_barrier(jnp.concatenate(pieces, 0))


def plus(a, b):
    return (a.astype(F32) + b.astype(F32)).astype(BF)


def scatter_chain(n_rows, early, late, axes):
    sizes = torus(n_rows)
    held = None
    for axis in axes[::-1]:
        n = sizes[axis]
        ahead, back = swap(n_rows, axis, 0), swap(n_rows, axis, 1)
        if held is not None:
            cut = held.shape[0] // n * max(n - 2, 1)
            early, late = held[:cut], held[cut:]
        size = (early.shape[0] + late.shape[0]) // n
        total = late
        first, second = early, late
        for step in range(n // 2 - 1, 0, -1):
            (got,) = yield [(total, BOTH, back if step % 2 else ahead)]
            kept = early[(2 * step - 2) * size : 2 * step * size]
            if step > 1:
                total = plus(got, kept)
            else:
                second = plus(got[size:], kept[size:])
                first = plus(got[:size], kept[:size])
        (got,) = yield [(second, BOTH, ahead)]
        held = first.astype(F32) + got.astype(F32)
        if axis != axes[0]:
            held = held.astype(BF)
    return held


def index_chain(block):
    (got,) = yield [(block, "rep", SWAP)]
    return jnp.concatenate([block, got], 1).reshape(-1)


def tile_chain(core, tiles, counts, group):
    (core,) = yield [core]
    own, send, *zeros = pack(core, tiles, counts, group)
    (send,) = yield [send]
    (other,) = yield [(send, "rep", SWAP)]
    return own, other, zeros


def sum_chain(n_rows, part):
    bit = 1
    while bit < n_rows:
        (got,) = yield [(part, "rows", tuple((i, i ^ bit) for i in range(n_rows)))]
        part = part + got
        bit *= 2
    (got,) = yield [(part, "rep", SWAP)]
    return part, got


def drive(chains, plan):
    asks = [next(c) for c in chains]
    flying = {}
    results = [None] * len(chains)

    def finish(names):
        names = [i for i in names if i in flying]
        if not names:
            return
        values = lax.optimization_barrier(tuple(tuple(flying.pop(i)) for i in names))
        for i, value in zip(names, values):
            try:
                asks[i] = chains[i].send(value)
            except StopIteration as stop:
                asks[i], results[i] = None, stop.value

    def start(names):
        for i in names:
            if asks[i] is not None and i not in flying:
                flying[i] = [lax.ppermute(*a) if isinstance(a, tuple) else a for a in asks[i]]

    for starts, ends in plan:
        start(starts)
        finish(ends)
    every = range(len(chains))
    while any(ask is not None for ask in asks):
        start(every)
        finish(every)
    return results


def late_sizes(n_rows, gathering):
    sizes = torus(n_rows)
    out = []
    for _, count, axes in PARTS:
        n = sizes[axes[-1]]
        out.append(count * n_rows // n * (1 if n == 2 or (n == 4 and gathering) else 2))
    return tuple(out)


def arranged(n_rows, place, late):
    base = 0
    tail = sum(count * n_rows for _, count, _ in PARTS) - sum(late)
    out = place
    for (first, count, _), last in zip(PARTS, late):
        early = count * n_rows - last
        inside = place - first * n_rows
        mine = (inside >= 0) & (inside < count * n_rows)
        at = jnp.where(inside < early, base + inside, tail + inside - early)
        out = jnp.where(mine, at, out)
        base += early
        tail += last
    return out


def copy_each(at, refs, start):
    low = 0
    for ref in refs:
        high = low + ref.shape[0]

        @pl.when((at >= low) & (at < high))
        def _(ref=ref, low=low):
            start(ref.at[at - low])

        low = high


def positions(n_rows, tile_rows, block, here, core):
    sizes = torus(n_rows)
    owner, local = block // tile_rows, block % tile_rows

    def split(i):
        return (i // (sizes[1] * sizes[2]), i // sizes[2] % sizes[1], i % sizes[2])

    mine, theirs = split(here), split(owner)
    slot = []
    for axis in range(3):
        n = sizes[axis]
        turn = jnp.where((mine[axis] + core) % 2 == 0, 1, -1)
        offset = (turn * (theirs[axis] - mine[axis]) + n) % n
        slot.append(sum(jnp.where(offset == e, i, 0) for i, e in enumerate(ARRIVAL[n])))
    place = jnp.zeros_like(block)
    for first, count, axes in PARTS:
        a, b, c = axes
        at = ((slot[c] * sizes[b] + slot[b]) * sizes[a] + slot[a]) * count + local - first
        place = jnp.where((local >= first) & (local < first + count), first * n_rows + at, place)
    return place


def pack_kernel(width, core_ref, tiles_ref, own_ref, send_ref, *zero_refs):
    side = tiles_ref.shape[2]
    half = side // 2
    for zero_ref in zero_refs:
        zero_ref[...] = jnp.zeros_like(zero_ref)

    def fill(first, second):
        for q in range(tiles_ref.shape[1] // width):
            group = [tiles_ref[0, q * width + i] for i in range(width)]
            first[0, q] = jnp.concatenate([t[:, :half] for t in group], 1)
            second[0, q] = jnp.concatenate([t[:, half:] for t in group], 1)

    @pl.when(core_ref[0] == 0)
    def _():
        fill(own_ref, send_ref)

    @pl.when(core_ref[0] != 0)
    def _():
        fill(send_ref, own_ref)


def pack(core, tiles, counts, width):
    rows, slots, side, _ = tiles.shape
    packed = jax.ShapeDtypeStruct((rows, slots // width, side, width * side // 2), BF)
    spec = pl.BlockSpec((1, slots // width, side, width * side // 2), lambda b: (b, 0, 0, 0))
    zeros = [jax.ShapeDtypeStruct((n, side // 2, side), BF) for n in counts]
    return pl.pallas_call(
        functools.partial(pack_kernel, width),
        grid=(rows,),
        in_specs=[
            pl.BlockSpec(memory_space=pltpu.SMEM),
            pl.BlockSpec((1, slots, side, side), lambda b: (b, 0, 0, 0)),
        ],
        out_specs=[
            spec,
            spec,
        ]
        + [pl.BlockSpec((n // rows, side // 2, side), lambda b: (b, 0, 0)) for n in counts],
        out_shape=[packed, packed] + zeros,
        compiler_params=pltpu.CompilerParams(vmem_limit_bytes=40 * 2**20),
        cost_estimate=pl.CostEstimate(flops=0, bytes_accessed=33 * 2**20, transcendentals=0),
        name="pack_tiles",
    )(core, tiles)


def forward_kernel(place_ref, own_ref, other_ref, *refs):
    *blocks, sum_ref, held, sems = refs
    b = pl.program_id(0)
    rows = pl.num_programs(0)
    slots = held.shape[1]
    half = held.shape[2]

    def fetch(row):
        slot = lax.rem(row, 2)

        @pl.loop(0, slots, unroll=8)
        def _(k):
            copy_each(
                place_ref[row * slots + k],
                blocks,
                lambda src: pltpu.make_async_copy(src, held.at[slot, k], sems.at[slot]).start(),
            )

    @pl.when(b == 0)
    def _():
        fetch(b)

    @pl.when(b + 1 < rows)
    def _():
        fetch(b + 1)

    now = lax.rem(b, 2)
    pltpu.make_async_copy(blocks[0].at[pl.ds(0, slots)], held.at[now], sems.at[now]).wait()
    total = jnp.zeros(sum_ref.shape[1:], F32)
    width = own_ref.shape[3] // half
    k = 0
    for ref in (own_ref, other_ref):
        for q in range(ref.shape[1]):
            right = held[now, k : k + width].reshape(width * half, -1)
            total += jnp.dot(ref[0, q], right, preferred_element_type=F32)
            k += width
    sum_ref[0] = total


def forward(place, own, other, blocks):
    rows, groups, side, wide = own.shape
    slots = place.shape[0] // rows
    spec = pl.BlockSpec((1, groups, side, wide), lambda b: (b, 0, 0, 0))
    return pl.pallas_call(
        forward_kernel,
        grid=(rows,),
        in_specs=[
            pl.BlockSpec(memory_space=pltpu.SMEM),
            spec,
            spec,
        ]
        + [pl.BlockSpec(memory_space=pl.ANY)] * len(blocks),
        out_specs=pl.BlockSpec((1, side, blocks[0].shape[2]), lambda b: (b, 0, 0)),
        out_shape=jax.ShapeDtypeStruct((rows, side, blocks[0].shape[2]), F32),
        scratch_shapes=[
            pltpu.VMEM((2, slots) + blocks[0].shape[1:], BF),
            pltpu.SemaphoreType.DMA((2,)),
        ],
        compiler_params=pltpu.CompilerParams(vmem_limit_bytes=40 * 2**20),
        cost_estimate=pl.CostEstimate(flops=2**30, bytes_accessed=2**24, transcendentals=0),
        name="forward_tiles",
    )(place, own, other, *blocks)


def backward_kernel(
    core_ref, place_ref, mine_ref, came_ref, weight_ref, cot_ref, own_ref, other_ref, *refs
):
    act_ref, wgrad_ref, *terms, held, sems = refs[(len(refs) - 4) // 2 :]
    b = pl.program_id(0)
    rows = pl.num_programs(0)
    slots = held.shape[1]
    half = held.shape[2]
    now = lax.rem(b, 2)

    def drain(slot):
        pltpu.make_async_copy(held.at[slot], terms[0].at[pl.ds(0, slots)], sems.at[slot]).wait()

    agg = (mine_ref[0] + came_ref[0]).astype(BF)
    weight = weight_ref[...]
    pre = jnp.dot(agg, weight, preferred_element_type=F32)
    sig = jax.nn.sigmoid(pre)
    act_ref[0] = (pre * sig).astype(BF)
    grad = (cot_ref[0].astype(F32) * sig * (1.0 + pre * (1.0 - sig))).astype(BF)
    spread = lax.dot_general(
        grad, weight, (((1,), (1,)), ((), ())), preferred_element_type=F32
    ).astype(BF)
    hid = grad.shape[1] // 2
    part = jnp.where(core_ref[0] == 0, grad[:, :hid].astype(F32), grad[:, hid:].astype(F32)).astype(BF)
    wgrad = lax.dot_general(agg, part, (((0,), (0,)), ((), ())), preferred_element_type=F32)

    @pl.when(b == 0)
    def _():
        wgrad_ref[...] = wgrad

    @pl.when(b > 0)
    def _():
        wgrad_ref[...] += wgrad

    @pl.when(b >= 2)
    def _():
        drain(now)

    width = own_ref.shape[3] // half
    k = 0
    for ref in (own_ref, other_ref):
        for q in range(ref.shape[1]):
            term = lax.dot_general(
                ref[0, q], spread, (((0,), (0,)), ((), ())), preferred_element_type=F32
            ).astype(BF)
            held[now, k : k + width] = term.reshape(width, half, -1)
            k += width

    @pl.loop(0, slots, unroll=8)
    def _(k):
        copy_each(
            place_ref[b * slots + k],
            terms,
            lambda dst: pltpu.make_async_copy(held.at[now, k], dst, sems.at[now]).start(),
        )

    @pl.when(b == rows - 1)
    def _():
        drain(lax.rem(b + 1, 2))
        drain(now)


def backward(core, place, mine, came, weight, cotangent, own, other, zeros):
    rows, groups, side, wide = own.shape
    slots = place.shape[0] // rows
    feat, hid = weight.shape
    tile_spec = pl.BlockSpec((1, groups, side, wide), lambda b: (b, 0, 0, 0))
    row_spec = pl.BlockSpec((1, side, feat), lambda b: (b, 0, 0))
    hid_spec = pl.BlockSpec((1, side, hid), lambda b: (b, 0, 0))
    smem = pl.BlockSpec(memory_space=pltpu.SMEM)
    return pl.pallas_call(
        backward_kernel,
        grid=(rows,),
        in_specs=[
            smem,
            smem,
            row_spec,
            row_spec,
            pl.BlockSpec((feat, hid), lambda b: (0, 0)),
            hid_spec,
            tile_spec,
            tile_spec,
        ]
        + [pl.BlockSpec(memory_space=pl.ANY)] * len(zeros),
        out_specs=[
            hid_spec,
            pl.BlockSpec((feat, hid // 2), lambda b: (0, 0)),
        ]
        + [pl.BlockSpec(memory_space=pl.ANY)] * len(zeros),
        out_shape=[
            jax.ShapeDtypeStruct((rows, side, hid), BF),
            jax.ShapeDtypeStruct((feat, hid // 2), F32),
        ]
        + [jax.ShapeDtypeStruct(z.shape, BF) for z in zeros],
        scratch_shapes=[
            pltpu.VMEM((2, slots) + zeros[0].shape[1:], BF),
            pltpu.SemaphoreType.DMA((2,)),
        ],
        input_output_aliases={8 + i: 2 + i for i in range(len(zeros))},
        compiler_params=pltpu.CompilerParams(vmem_limit_bytes=40 * 2**20),
        cost_estimate=pl.CostEstimate(flops=2**30, bytes_accessed=2**24, transcendentals=2**18),
        name="backward_tiles",
    )(core, place, mine, came, weight, cotangent, own, other, *zeros)


def body(features, weight, tiles, tile_cols, order, cotangent):
    tile_rows, row_slots, side, _ = tiles.shape
    width = features.shape[1]
    n_tiles = order.shape[0]
    n_rows = lax.axis_size("rows")
    here = lax.axis_index("rows")
    core = lax.axis_index("rep")
    core_ref = core.reshape(1).astype(jnp.int32)
    half = side // 2
    group = 4 if row_slots % 4 == 0 else 2

    halves = features.reshape(tile_rows, 2, half, width)
    own_half = jnp.where(core == 0, halves[:, 0], halves[:, 1])
    labels = jnp.arange(n_tiles, dtype=jnp.int32)
    flat = tile_cols.reshape(-1)
    block = jnp.sum(jnp.where(flat[:, None] == labels[None, :], order[None, :], 0), axis=1)
    block = block.reshape(tile_rows, row_slots)
    last, first = late_sizes(n_rows, True), late_sizes(n_rows, False)

    three = (0, 1, 2)
    rounds = ((three, three),) * 4 + (
        ((1, 2, 0), (1, 2)),
        ((1, 2, 3), (0, 1, 2, 3)),
        ((0, 1, 2, 4), (0, 4)),
        ((0, 4), (0, 1, 2, 4)),
        ((0, 1, 2, 4), (0, 1, 2, 4)),
    )
    chains = [gather_chain(n_rows, own_half[f : f + c], axes) for f, c, axes in PARTS]
    chains.append(index_chain(block))
    chains.append(tile_chain(core_ref, tiles, (n_tiles - sum(first),) + first, group))
    *pieces, block, (own, other, zeros) = drive(chains, rounds if n_rows == 128 else ())
    gathered = [jnp.concatenate([p for part in pieces for p in part[:-1]], 0)]
    gathered += [part[-1] for part in pieces]
    place = positions(n_rows, tile_rows, block, here, core)

    mine = forward(arranged(n_rows, place, last), own, other, gathered)
    came = lax.ppermute(mine, "rep", SWAP)
    activated, wgrad, early, *late = backward(
        core_ref, arranged(n_rows, place, first), mine, came, weight,
        cotangent.reshape(tile_rows, side, -1), own, other, zeros,
    )

    every = (0, 1, 2, 3)
    rounds = (
        (every, (3,)),
        ((3,), every),
        (every, (3,)),
        ((3,), (0, 3)),
        ((0, 3), (3,)),
        ((3,), every),
        (every, (1, 2, 3)),
        ((1, 2, 3), every),
    )
    chains = []
    base = 0
    for (_, count, axes), out in zip(PARTS, late):
        size = count * n_rows - out.shape[0]
        chains.append(scatter_chain(n_rows, early[base : base + size], out, axes))
        base += size
    *owned, (wgrad, wother) = drive(
        chains + [sum_chain(n_rows, wgrad)], rounds if n_rows == 128 else ()
    )
    weight_grad = jnp.where(
        core == 0, jnp.concatenate([wgrad, wother], 1), jnp.concatenate([wother, wgrad], 1)
    )
    owned = jnp.concatenate(owned, 0)
    pair = lax.ppermute(owned, "rep", SWAP)
    feature_grad = jnp.where(
        core == 0, jnp.stack([owned, pair], 1), jnp.stack([pair, owned], 1)
    ).reshape(tile_rows * side, width)
    return activated.reshape(tile_rows * side, -1), feature_grad, weight_grad


def solution(mesh):
    in_specs = (
        P("rows", None),
        P(),
        P("rows", "rep", None, None),
        P("rows", "rep"),
        P(),
        P("rows", None),
    )
    out_specs = (P("rows", None), P("rows", None), P())
    return jax.shard_map(body, mesh=mesh, in_specs=in_specs, out_specs=out_specs, check_vma=False)
```

```python
import functools

import jax
import jax.numpy as jnp
from jax import lax
from jax.experimental import pallas as pl
from jax.experimental.pallas import tpu as pltpu
from jax.sharding import PartitionSpec as P

BF = jnp.bfloat16
F32 = jnp.float32
BOTH = ("rows", "rep")
SWAP = ((0, 1), (1, 0))


def torus(n_rows):
    return {128: (4, 8, 4), 8: (2, 2, 2)}[n_rows]


def swap(n_rows, axis, turn):
    sizes = torus(n_rows)
    pairs = []
    for i in range(n_rows):
        c = [i // (sizes[1] * sizes[2]), i // sizes[2] % sizes[1], i % sizes[2]]
        for core in range(2):
            t = list(c)
            t[axis] = (t[axis] + (1 if (t[axis] + core + turn) % 2 == 0 else -1)) % sizes[axis]
            pairs.append((2 * i + core, 2 * ((t[0] * sizes[1] + t[1]) * sizes[2] + t[2]) + core))
    return tuple(pairs)


PARTS = ((0, 2, (2, 0, 1)), (2, 3, (1, 0, 2)), (5, 3, (1, 2, 0)))
ARRIVAL = {2: (0, 1), 4: (0, 1, 3, 2), 8: (0, 1, 7, 6, 2, 3, 5, 4)}


def together(chains):
    asks = [next(c) for c in chains]
    results = [None] * len(chains)
    while any(ask is not None for ask in asks):
        came = yield [a for ask in asks if ask is not None for a in ask]
        for i, chain in enumerate(chains):
            if asks[i] is None:
                continue
            mine, came = came[: len(asks[i])], came[len(asks[i]) :]
            try:
                asks[i] = chain.send(mine)
            except StopIteration as stop:
                asks[i], results[i] = None, stop.value
    return results


def gather_pair(n_rows, own, parts):
    (_, count, (axis, *_)), (_, more, _) = parts
    held = yield from gather_chain(n_rows, own, (axis,), False)
    held = held.reshape((-1, count + more) + held.shape[1:])
    split = (held[:, :count], held[:, count:])
    split = [h.reshape((-1,) + own.shape[1:]) for h in split]
    chains = [gather_chain(n_rows, h, axes[1:]) for h, (_, _, axes) in zip(split, parts)]
    return (yield from together(chains))


def gather_chain(n_rows, own, axes, spread=True):
    sizes = torus(n_rows)
    held = own
    for axis in axes:
        n = sizes[axis]
        ahead, back = swap(n_rows, axis, 0), swap(n_rows, axis, 1)
        if spread and axis == axes[-1] and n == 4:
            one, two = yield [(held, BOTH, ahead), (held, BOTH, back)]
            (far,) = yield [(one, BOTH, back)]
            return [held, one, two, far]
        pieces = [held]
        send = held
        for step in range(n // 2):
            (got,) = yield [(send, BOTH, back if step % 2 else ahead)]
            pieces.append(got)
            send = jnp.concatenate([held, got], 0) if step == 0 else got
        if spread and axis == axes[-1]:
            return pieces
        held = lax.optimization_barrier(jnp.concatenate(pieces, 0))
    return held


def plus(a, b):
    return (a.astype(F32) + b.astype(F32)).astype(BF)


def scatter_pair(n_rows, buffers, parts):
    (_, count, (axis, *_)), (_, more, _) = parts
    chains = [
        scatter_chain(n_rows, early, late, axes[1:], False)
        for (early, late), (_, _, axes) in zip(buffers, parts)
    ]
    a, b = yield from together(chains)
    n = torus(n_rows)[axis]
    held = jnp.concatenate(
        [a.reshape((n, count) + a.shape[1:]), b.reshape((n, more) + b.shape[1:])], 1
    ).reshape((-1,) + a.shape[1:])
    cut = (count + more) * max(n - 2, 1)
    return (yield from scatter_chain(n_rows, held[:cut], held[cut:], (axis,)))


def scatter_chain(n_rows, early, late, axes, done=True):
    sizes = torus(n_rows)
    held = None
    for axis in axes[::-1]:
        n = sizes[axis]
        ahead, back = swap(n_rows, axis, 0), swap(n_rows, axis, 1)
        if held is not None:
            cut = held.shape[0] // n * max(n - 2, 1)
            early, late = held[:cut], held[cut:]
        size = (early.shape[0] + late.shape[0]) // n
        total = late
        first, second = early, late
        for step in range(n // 2 - 1, 0, -1):
            (got,) = yield [(total, BOTH, back if step % 2 else ahead)]
            kept = early[(2 * step - 2) * size : 2 * step * size]
            if step > 1:
                total = plus(got, kept)
            else:
                second = plus(got[size:], kept[size:])
                first = plus(got[:size], kept[:size])
        (got,) = yield [(second, BOTH, ahead)]
        held = first.astype(F32) + got.astype(F32)
        if axis != axes[0] or not done:
            held = held.astype(BF)
    return held


def index_chain(block):
    (got,) = yield [(block, "rep", SWAP)]
    return jnp.concatenate([block, got], 1).reshape(-1)


def tile_chain(core, tiles, group):
    (core,) = yield [core]
    own, send = pack(core, tiles, group)
    (send,) = yield [send]
    (other,) = yield [(send, "rep", SWAP)]
    return own, other


def sum_chain(n_rows, part):
    bit = 1
    while bit < n_rows:
        (got,) = yield [(part, "rows", tuple((i, i ^ bit) for i in range(n_rows)))]
        part = part + got
        bit *= 2
    (got,) = yield [(part, "rep", SWAP)]
    return part, got


def drive(chains, plan):
    asks = [next(c) for c in chains]
    flying = {}
    results = [None] * len(chains)

    def finish(names):
        names = [i for i in names if i in flying]
        if not names:
            return
        values = lax.optimization_barrier(tuple(tuple(flying.pop(i)) for i in names))
        for i, value in zip(names, values):
            try:
                asks[i] = chains[i].send(value)
            except StopIteration as stop:
                asks[i], results[i] = None, stop.value

    def start(names):
        for i in names:
            if asks[i] is not None and i not in flying:
                flying[i] = [lax.ppermute(*a) if isinstance(a, tuple) else a for a in asks[i]]

    for starts, ends in plan:
        start(starts)
        finish(ends)
    every = range(len(chains))
    while any(ask is not None for ask in asks):
        start(every)
        finish(every)
    return results


def late_sizes(n_rows, gathering):
    sizes = torus(n_rows)
    out = []
    for _, count, axes in PARTS:
        n = sizes[axes[-1]]
        out.append(count * n_rows // n * (1 if n == 2 or (n == 4 and gathering) else 2))
    return tuple(out)


def arranged(n_rows, place, late):
    base = 0
    tail = sum(count * n_rows for _, count, _ in PARTS) - sum(late)
    out = place
    for (first, count, _), last in zip(PARTS, late):
        early = count * n_rows - last
        inside = place - first * n_rows
        mine = (inside >= 0) & (inside < count * n_rows)
        at = jnp.where(inside < early, base + inside, tail + inside - early)
        out = jnp.where(mine, at, out)
        base += early
        tail += last
    return out


def copy_each(at, refs, start, low=0):
    high = low + refs[0].shape[0]
    if len(refs) == 1:
        start(refs[0].at[at - low])
        return
    lax.cond(
        at < high,
        lambda: start(refs[0].at[at - low]),
        lambda: copy_each(at, refs[1:], start, high),
    )


def positions(n_rows, tile_rows, block, here, core):
    sizes = torus(n_rows)
    owner, local = block // tile_rows, block % tile_rows

    def split(i):
        return (i // (sizes[1] * sizes[2]), i // sizes[2] % sizes[1], i % sizes[2])

    mine, theirs = split(here), split(owner)
    slot = []
    for axis in range(3):
        n = sizes[axis]
        turn = jnp.where((mine[axis] + core) % 2 == 0, 1, -1)
        offset = (turn * (theirs[axis] - mine[axis]) + n) % n
        slot.append(sum(jnp.where(offset == e, i, 0) for i, e in enumerate(ARRIVAL[n])))
    place = jnp.zeros_like(block)
    for first, count, axes in PARTS:
        a, b, c = axes
        at = ((slot[c] * sizes[b] + slot[b]) * sizes[a] + slot[a]) * count + local - first
        place = jnp.where((local >= first) & (local < first + count), first * n_rows + at, place)
    return place


def pack_kernel(width, core_ref, tiles_ref, own_ref, send_ref):
    side = tiles_ref.shape[2]
    half = side // 2

    def fill(first, second):
        for q in range(tiles_ref.shape[1] // width):
            group = [tiles_ref[0, q * width + i] for i in range(width)]
            first[0, q] = jnp.concatenate([t[:, :half] for t in group], 1)
            second[0, q] = jnp.concatenate([t[:, half:] for t in group], 1)

    @pl.when(core_ref[0] == 0)
    def _():
        fill(own_ref, send_ref)

    @pl.when(core_ref[0] != 0)
    def _():
        fill(send_ref, own_ref)


def pack(core, tiles, width):
    rows, slots, side, _ = tiles.shape
    packed = jax.ShapeDtypeStruct((rows, slots // width, side, width * side // 2), BF)
    spec = pl.BlockSpec((1, slots // width, side, width * side // 2), lambda b: (b, 0, 0, 0))
    return pl.pallas_call(
        functools.partial(pack_kernel, width),
        grid=(rows,),
        in_specs=[
            pl.BlockSpec(memory_space=pltpu.SMEM),
            pl.BlockSpec((1, slots, side, side), lambda b: (b, 0, 0, 0)),
        ],
        out_specs=[
            spec,
            spec,
        ],
        out_shape=[packed, packed],
        compiler_params=pltpu.CompilerParams(vmem_limit_bytes=40 * 2**20),
        cost_estimate=pl.CostEstimate(flops=0, bytes_accessed=2**24, transcendentals=0),
        name="pack_tiles",
    )(core, tiles)


def forward_kernel(place_ref, own_ref, other_ref, *refs):
    *blocks, sum_ref, held, sems = refs
    b = pl.program_id(0)
    rows = pl.num_programs(0)
    slots = held.shape[1]
    half = held.shape[2]

    def fetch(row):
        slot = lax.rem(row, 2)

        @pl.loop(0, slots, unroll=8)
        def _(k):
            copy_each(
                place_ref[row * slots + k],
                blocks,
                lambda src: pltpu.make_async_copy(src, held.at[slot, k], sems.at[slot]).start(),
            )

    @pl.when(b == 0)
    def _():
        fetch(b)

    @pl.when(b + 1 < rows)
    def _():
        fetch(b + 1)

    now = lax.rem(b, 2)
    pltpu.make_async_copy(blocks[0].at[pl.ds(0, slots)], held.at[now], sems.at[now]).wait()
    total = jnp.zeros(sum_ref.shape[1:], F32)
    width = own_ref.shape[3] // half
    k = 0
    for ref in (own_ref, other_ref):
        for q in range(ref.shape[1]):
            right = held[now, k : k + width].reshape(width * half, -1)
            total += jnp.dot(ref[0, q], right, preferred_element_type=F32)
            k += width
    sum_ref[0] = total


def forward(place, own, other, blocks):
    rows, groups, side, wide = own.shape
    slots = place.shape[0] // rows
    spec = pl.BlockSpec((1, groups, side, wide), lambda b: (b, 0, 0, 0))
    return pl.pallas_call(
        forward_kernel,
        grid=(rows,),
        in_specs=[
            pl.BlockSpec(memory_space=pltpu.SMEM),
            spec,
            spec,
        ]
        + [pl.BlockSpec(memory_space=pl.ANY)] * len(blocks),
        out_specs=pl.BlockSpec((1, side, blocks[0].shape[2]), lambda b: (b, 0, 0)),
        out_shape=jax.ShapeDtypeStruct((rows, side, blocks[0].shape[2]), F32),
        scratch_shapes=[
            pltpu.VMEM((2, slots) + blocks[0].shape[1:], BF),
            pltpu.SemaphoreType.DMA((2,)),
        ],
        compiler_params=pltpu.CompilerParams(vmem_limit_bytes=40 * 2**20),
        cost_estimate=pl.CostEstimate(flops=2**30, bytes_accessed=2**24, transcendentals=0),
        name="forward_tiles",
    )(place, own, other, *blocks)


def backward_kernel(
    core_ref, place_ref, mine_ref, came_ref, weight_ref, cot_ref, own_ref, other_ref, *refs
):
    act_ref, wgrad_ref, *terms, held, sems = refs
    b = pl.program_id(0)
    rows = pl.num_programs(0)
    half = held.shape[1]

    @pl.when(b == 0)
    def _():
        @pl.loop(0, held.shape[0] // 8)
        def _(i):
            held[pl.ds(i * 8, 8)] = jnp.zeros((8,) + held.shape[1:], BF)

    agg = (mine_ref[0] + came_ref[0]).astype(BF)
    weight = weight_ref[...]
    pre = jnp.dot(agg, weight, preferred_element_type=F32)
    sig = jax.nn.sigmoid(pre)
    act_ref[0] = (pre * sig).astype(BF)
    grad = (cot_ref[0].astype(F32) * sig * (1.0 + pre * (1.0 - sig))).astype(BF)
    spread = lax.dot_general(
        grad, weight, (((1,), (1,)), ((), ())), preferred_element_type=F32
    ).astype(BF)
    hid = grad.shape[1] // 2
    part = jnp.where(core_ref[0] == 0, grad[:, :hid].astype(F32), grad[:, hid:].astype(F32)).astype(BF)
    wgrad = lax.dot_general(agg, part, (((0,), (0,)), ((), ())), preferred_element_type=F32)

    @pl.when(b == 0)
    def _():
        wgrad_ref[...] = wgrad

    @pl.when(b > 0)
    def _():
        wgrad_ref[...] += wgrad

    width = own_ref.shape[3] // half
    k = b * (place_ref.shape[0] // rows)
    for ref in (own_ref, other_ref):
        for q in range(ref.shape[1]):
            term = lax.dot_general(
                ref[0, q], spread, (((0,), (0,)), ((), ())), preferred_element_type=F32
            ).astype(BF)
            for i in range(width):
                held[place_ref[k + i]] = term[i * half : (i + 1) * half]
            k += width

    @pl.when(b == rows - 1)
    def _():
        copies = []
        low = 0
        for i, out in enumerate(terms):
            size = out.shape[0]
            copies.append(pltpu.make_async_copy(held.at[pl.ds(low, size)], out, sems.at[i]))
            low += size
        for copy in copies:
            copy.start()
        for copy in copies:
            copy.wait()


def backward(core, place, mine, came, weight, cotangent, own, other, counts):
    rows, groups, side, wide = own.shape
    feat, hid = weight.shape
    tile_spec = pl.BlockSpec((1, groups, side, wide), lambda b: (b, 0, 0, 0))
    row_spec = pl.BlockSpec((1, side, feat), lambda b: (b, 0, 0))
    hid_spec = pl.BlockSpec((1, side, hid), lambda b: (b, 0, 0))
    smem = pl.BlockSpec(memory_space=pltpu.SMEM)
    return pl.pallas_call(
        backward_kernel,
        grid=(rows,),
        in_specs=[
            smem,
            smem,
            row_spec,
            row_spec,
            pl.BlockSpec((feat, hid), lambda b: (0, 0)),
            hid_spec,
            tile_spec,
            tile_spec,
        ],
        out_specs=[
            hid_spec,
            pl.BlockSpec((feat, hid // 2), lambda b: (0, 0)),
        ]
        + [pl.BlockSpec(memory_space=pl.ANY)] * len(counts),
        out_shape=[
            jax.ShapeDtypeStruct((rows, side, hid), BF),
            jax.ShapeDtypeStruct((feat, hid // 2), F32),
        ]
        + [jax.ShapeDtypeStruct((n, side // 2, feat), BF) for n in counts],
        scratch_shapes=[
            pltpu.VMEM((sum(counts), side // 2, feat), BF),
            pltpu.SemaphoreType.DMA((len(counts),)),
        ],
        compiler_params=pltpu.CompilerParams(vmem_limit_bytes=40 * 2**20),
        cost_estimate=pl.CostEstimate(flops=2**30, bytes_accessed=2**24, transcendentals=2**18),
        name="backward_tiles",
    )(core, place, mine, came, weight, cotangent, own, other)


def body(features, weight, tiles, tile_cols, order, cotangent):
    tile_rows, row_slots, side, _ = tiles.shape
    width = features.shape[1]
    n_tiles = order.shape[0]
    n_rows = lax.axis_size("rows")
    here = lax.axis_index("rows")
    core = lax.axis_index("rep")
    core_ref = core.reshape(1).astype(jnp.int32)
    half = side // 2
    group = 4 if row_slots % 4 == 0 else 2

    halves = features.reshape(tile_rows, 2, half, width)
    own_half = jnp.where(core == 0, halves[:, 0], halves[:, 1])
    labels = jnp.arange(n_tiles, dtype=jnp.int32)
    flat = tile_cols.reshape(-1)
    block = jnp.sum(jnp.where(flat[:, None] == labels[None, :], order[None, :], 0), axis=1)
    block = block.reshape(tile_rows, row_slots)
    last, first = late_sizes(n_rows, True), late_sizes(n_rows, False)

    rounds = (((0, 1), (0, 1)),) * 4 + (
        ((1, 0), (1,)),
        ((1, 2), (0, 1, 2)),
        ((0, 1, 3), (0, 3)),
        ((0, 3), (0, 1, 3)),
        ((0, 1, 3), (0, 1, 3)),
    )
    single, pair = PARTS[0], PARTS[1:]
    chains = [
        gather_chain(n_rows, own_half[: single[1]], single[2]),
        gather_pair(n_rows, own_half[single[1] :], pair),
        index_chain(block),
        tile_chain(core_ref, tiles, group),
    ]
    pieces, pieces_pair, block, (own, other) = drive(chains, rounds if n_rows == 128 else ())
    pieces = [pieces, *pieces_pair]
    gathered = [jnp.concatenate([p for part in pieces for p in part[:-1]], 0)]
    gathered += [part[-1] for part in pieces]
    place = positions(n_rows, tile_rows, block, here, core)

    mine = forward(arranged(n_rows, place, last), own, other, gathered)
    came = lax.ppermute(mine, "rep", SWAP)
    activated, wgrad, early, *late = backward(
        core_ref, arranged(n_rows, place, first), mine, came, weight,
        cotangent.reshape(tile_rows, side, -1), own, other, (n_tiles - sum(first),) + first,
    )

    every = (0, 1, 2)
    rounds = (
        (every, (2,)),
        ((2,), (2,)),
        ((2,), (0, 2)),
        ((2,), (2,)),
        ((2,), every),
        (every, (2,)),
        ((2,), (0, 2)),
        ((0, 2), every),
        ((0, 1), (1,)),
        ((1,), (0, 1)),
    )
    buffers = []
    base = 0
    for (_, count, axes), out in zip(PARTS, late):
        size = count * n_rows - out.shape[0]
        buffers.append((early[base : base + size], out))
        base += size
    chains = [
        scatter_chain(n_rows, *buffers[0], single[2]),
        scatter_pair(n_rows, buffers[1:], pair),
        sum_chain(n_rows, wgrad),
    ]
    *owned, (wgrad, wother) = drive(chains, rounds if n_rows == 128 else ())
    weight_grad = jnp.where(
        core == 0, jnp.concatenate([wgrad, wother], 1), jnp.concatenate([wother, wgrad], 1)
    )
    owned = jnp.concatenate(owned, 0)
    across = lax.ppermute(owned, "rep", SWAP)
    feature_grad = jnp.where(
        core == 0, jnp.stack([owned, across], 1), jnp.stack([across, owned], 1)
    ).reshape(tile_rows * side, width)
    return activated.reshape(tile_rows * side, -1), feature_grad, weight_grad


def solution(mesh):
    in_specs = (
        P("rows", None),
        P(),
        P("rows", "rep", None, None),
        P("rows", "rep"),
        P(),
        P("rows", None),
    )
    out_specs = (P("rows", None), P("rows", None), P())
    return jax.shard_map(body, mesh=mesh, in_specs=in_specs, out_specs=out_specs, check_vma=False)
```

```python
import functools

import jax
import jax.numpy as jnp
from jax import lax
from jax.experimental import pallas as pl
from jax.experimental.pallas import tpu as pltpu
from jax.sharding import PartitionSpec as P

BF = jnp.bfloat16
F32 = jnp.float32
BOTH = ("rows", "rep")
SWAP = ((0, 1), (1, 0))


def torus(n_rows):
    return {128: (4, 8, 4), 8: (2, 2, 2)}[n_rows]


def swap(n_rows, axis, turn):
    sizes = torus(n_rows)
    pairs = []
    for i in range(n_rows):
        c = [i // (sizes[1] * sizes[2]), i // sizes[2] % sizes[1], i % sizes[2]]
        for core in range(2):
            t = list(c)
            t[axis] = (t[axis] + (1 if (t[axis] + core + turn) % 2 == 0 else -1)) % sizes[axis]
            pairs.append((2 * i + core, 2 * ((t[0] * sizes[1] + t[1]) * sizes[2] + t[2]) + core))
    return tuple(pairs)


PARTS = ((0, 2, (2, 0, 1)), (2, 3, (1, 0, 2)), (5, 3, (1, 2, 0)))
ARRIVAL = {2: (0, 1), 4: (0, 1, 3, 2), 8: (0, 1, 7, 6, 2, 3, 5, 4)}


def together(chains):
    asks = [next(c) for c in chains]
    results = [None] * len(chains)
    while any(ask is not None for ask in asks):
        came = yield [a for ask in asks if ask is not None for a in ask]
        for i, chain in enumerate(chains):
            if asks[i] is None:
                continue
            mine, came = came[: len(asks[i])], came[len(asks[i]) :]
            try:
                asks[i] = chain.send(mine)
            except StopIteration as stop:
                asks[i], results[i] = None, stop.value
    return results


def gather_pair(n_rows, own, parts):
    (_, count, (axis, *_)), (_, more, _) = parts
    held = yield from gather_chain(n_rows, own, (axis,), False)
    held = held.reshape((-1, count + more) + held.shape[1:])
    split = (held[:, :count], held[:, count:])
    split = [h.reshape((-1,) + own.shape[1:]) for h in split]
    chains = [gather_chain(n_rows, h, axes[1:]) for h, (_, _, axes) in zip(split, parts)]
    return (yield from together(chains))


def gather_chain(n_rows, own, axes, spread=True):
    sizes = torus(n_rows)
    held = own
    for axis in axes:
        n = sizes[axis]
        ahead, back = swap(n_rows, axis, 0), swap(n_rows, axis, 1)
        if spread and axis == axes[-1] and n == 4:
            one, two = yield [(held, BOTH, ahead), (held, BOTH, back)]
            (far,) = yield [(one, BOTH, back)]
            return [held, one, two, far]
        pieces = [held]
        send = held
        for step in range(n // 2):
            (got,) = yield [(send, BOTH, back if step % 2 else ahead)]
            pieces.append(got)
            send = jnp.concatenate([held, got], 0) if step == 0 else got
        if spread and axis == axes[-1]:
            return pieces
        held = lax.optimization_barrier(jnp.concatenate(pieces, 0))
    return held


def plus(a, b):
    return (a.astype(F32) + b.astype(F32)).astype(BF)


def scatter_pair(n_rows, buffers, parts):
    (_, count, (axis, *_)), (_, more, _) = parts
    chains = [
        scatter_chain(n_rows, early, late, axes[1:], False)
        for (early, late), (_, _, axes) in zip(buffers, parts)
    ]
    a, b = yield from together(chains)
    n = torus(n_rows)[axis]
    held = jnp.concatenate(
        [a.reshape((n, count) + a.shape[1:]), b.reshape((n, more) + b.shape[1:])], 1
    ).reshape((-1,) + a.shape[1:])
    cut = (count + more) * max(n - 2, 1)
    return (yield from scatter_chain(n_rows, held[:cut], held[cut:], (axis,)))


def scatter_chain(n_rows, early, late, axes, done=True):
    sizes = torus(n_rows)
    held = None
    for axis in axes[::-1]:
        n = sizes[axis]
        ahead, back = swap(n_rows, axis, 0), swap(n_rows, axis, 1)
        if held is not None:
            cut = held.shape[0] // n * max(n - 2, 1)
            early, late = held[:cut], held[cut:]
        size = (early.shape[0] + late.shape[0]) // n
        total = late
        first, second = early, late
        for step in range(n // 2 - 1, 0, -1):
            (got,) = yield [(total, BOTH, back if step % 2 else ahead)]
            kept = early[(2 * step - 2) * size : 2 * step * size]
            if step > 1:
                total = plus(got, kept)
            else:
                second = plus(got[size:], kept[size:])
                first = plus(got[:size], kept[:size])
        (got,) = yield [(second, BOTH, ahead)]
        held = first.astype(F32) + got.astype(F32)
        if axis != axes[0] or not done:
            held = held.astype(BF)
    return held


def index_chain(block):
    (got,) = yield [(block, "rep", SWAP)]
    return jnp.concatenate([block, got], 1).reshape(-1)


def tile_chain(core, tiles, group):
    (core,) = yield [core]
    own, send = pack(core, tiles, group)
    (send,) = yield [send]
    (other,) = yield [(send, "rep", SWAP)]
    return own, other


def sum_chain(n_rows, part):
    bit = 1
    while bit < n_rows:
        (got,) = yield [(part, "rows", tuple((i, i ^ bit) for i in range(n_rows)))]
        part = part + got
        bit *= 2
    (got,) = yield [(part, "rep", SWAP)]
    return part, got


def drive(chains, plan):
    asks = [next(c) for c in chains]
    flying = {}
    results = [None] * len(chains)

    def finish(names):
        names = [i for i in names if i in flying]
        if not names:
            return
        values = lax.optimization_barrier(tuple(tuple(flying.pop(i)) for i in names))
        for i, value in zip(names, values):
            try:
                asks[i] = chains[i].send(value)
            except StopIteration as stop:
                asks[i], results[i] = None, stop.value

    def start(names):
        for i in names:
            if asks[i] is not None and i not in flying:
                flying[i] = [lax.ppermute(*a) if isinstance(a, tuple) else a for a in asks[i]]

    for starts, ends in plan:
        start(starts)
        finish(ends)
    every = range(len(chains))
    while any(ask is not None for ask in asks):
        start(every)
        finish(every)
    return results


def late_sizes(n_rows):
    sizes = torus(n_rows)
    out = []
    for _, count, axes in PARTS:
        n = sizes[axes[-1]]
        out.append(count * n_rows // n * (1 if n == 2 else 2))
    return tuple(out)


def arranged(n_rows, place, late):
    base = 0
    tail = sum(count * n_rows for _, count, _ in PARTS) - sum(late)
    out = place
    for (first, count, _), last in zip(PARTS, late):
        early = count * n_rows - last
        inside = place - first * n_rows
        mine = (inside >= 0) & (inside < count * n_rows)
        at = jnp.where(inside < early, base + inside, tail + inside - early)
        out = jnp.where(mine, at, out)
        base += early
        tail += last
    return out


def positions(n_rows, tile_rows, block, here, core):
    sizes = torus(n_rows)
    owner, local = block // tile_rows, block % tile_rows

    def split(i):
        return (i // (sizes[1] * sizes[2]), i // sizes[2] % sizes[1], i % sizes[2])

    mine, theirs = split(here), split(owner)
    slot = []
    for axis in range(3):
        n = sizes[axis]
        turn = jnp.where((mine[axis] + core) % 2 == 0, 1, -1)
        offset = (turn * (theirs[axis] - mine[axis]) + n) % n
        slot.append(sum(jnp.where(offset == e, i, 0) for i, e in enumerate(ARRIVAL[n])))
    place = jnp.zeros_like(block)
    for first, count, axes in PARTS:
        a, b, c = axes
        at = ((slot[c] * sizes[b] + slot[b]) * sizes[a] + slot[a]) * count + local - first
        place = jnp.where((local >= first) & (local < first + count), first * n_rows + at, place)
    return place


def pack_kernel(width, core_ref, tiles_ref, own_ref, send_ref):
    side = tiles_ref.shape[2]
    half = side // 2

    def fill(first, second):
        for q in range(tiles_ref.shape[1] // width):
            group = [tiles_ref[0, q * width + i] for i in range(width)]
            first[0, q] = jnp.concatenate([t[:, :half] for t in group], 1)
            second[0, q] = jnp.concatenate([t[:, half:] for t in group], 1)

    @pl.when(core_ref[0] == 0)
    def _():
        fill(own_ref, send_ref)

    @pl.when(core_ref[0] != 0)
    def _():
        fill(send_ref, own_ref)


def pack(core, tiles, width):
    rows, slots, side, _ = tiles.shape
    packed = jax.ShapeDtypeStruct((rows, slots // width, side, width * side // 2), BF)
    spec = pl.BlockSpec((1, slots // width, side, width * side // 2), lambda b: (b, 0, 0, 0))
    return pl.pallas_call(
        functools.partial(pack_kernel, width),
        grid=(rows,),
        in_specs=[
            pl.BlockSpec(memory_space=pltpu.SMEM),
            pl.BlockSpec((1, slots, side, side), lambda b: (b, 0, 0, 0)),
        ],
        out_specs=[
            spec,
            spec,
        ],
        out_shape=[packed, packed],
        compiler_params=pltpu.CompilerParams(vmem_limit_bytes=40 * 2**20),
        cost_estimate=pl.CostEstimate(flops=0, bytes_accessed=2**24, transcendentals=0),
        name="pack_tiles",
    )(core, tiles)


def forward_kernel(place_ref, own_ref, other_ref, *refs):
    *pieces, sum_ref, held, sems = refs
    b = pl.program_id(0)
    half = held.shape[1]

    @pl.when(b == 0)
    def _():
        copies = []
        low = 0
        for i, piece in enumerate(pieces):
            size = piece.shape[0]
            copies.append(pltpu.make_async_copy(piece, held.at[pl.ds(low, size)], sems.at[i]))
            low += size
        for copy in copies:
            copy.start()
        for copy in copies:
            copy.wait()

    total = jnp.zeros(sum_ref.shape[1:], F32)
    width = own_ref.shape[3] // half
    k = b * (place_ref.shape[0] // pl.num_programs(0))
    for ref in (own_ref, other_ref):
        for q in range(ref.shape[1]):
            right = jnp.concatenate([held[place_ref[k + i]] for i in range(width)], 0)
            total += jnp.dot(ref[0, q], right, preferred_element_type=F32)
            k += width
    sum_ref[0] = total


def forward(place, own, other, pieces):
    rows, groups, side, wide = own.shape
    n_tiles = sum(p.shape[0] for p in pieces)
    half, width = pieces[0].shape[1:]
    spec = pl.BlockSpec((1, groups, side, wide), lambda b: (b, 0, 0, 0))
    return pl.pallas_call(
        forward_kernel,
        grid=(rows,),
        in_specs=[pl.BlockSpec(memory_space=pltpu.SMEM), spec, spec]
        + [pl.BlockSpec(memory_space=pl.ANY)] * len(pieces),
        out_specs=pl.BlockSpec((1, side, width), lambda b: (b, 0, 0)),
        out_shape=jax.ShapeDtypeStruct((rows, side, width), F32),
        scratch_shapes=[
            pltpu.VMEM((n_tiles, half, width), BF),
            pltpu.SemaphoreType.DMA((len(pieces),)),
        ],
        compiler_params=pltpu.CompilerParams(vmem_limit_bytes=40 * 2**20),
        cost_estimate=pl.CostEstimate(flops=2**30, bytes_accessed=3 * 2**23, transcendentals=0),
        name="forward_tiles",
    )(place, own, other, *pieces)


def backward_kernel(
    core_ref, place_ref, mine_ref, came_ref, weight_ref, cot_ref, own_ref, other_ref, *refs
):
    act_ref, wgrad_ref, *terms, held, sems = refs
    b = pl.program_id(0)
    rows = pl.num_programs(0)
    half = held.shape[1]

    @pl.when(b == 0)
    def _():
        @pl.loop(0, held.shape[0] // 8)
        def _(i):
            held[pl.ds(i * 8, 8)] = jnp.zeros((8,) + held.shape[1:], BF)

    agg = (mine_ref[0] + came_ref[0]).astype(BF)
    weight = weight_ref[...]
    pre = jnp.dot(agg, weight, preferred_element_type=F32)
    sig = jax.nn.sigmoid(pre)
    act_ref[0] = (pre * sig).astype(BF)
    grad = (cot_ref[0].astype(F32) * sig * (1.0 + pre * (1.0 - sig))).astype(BF)
    spread = lax.dot_general(
        grad, weight, (((1,), (1,)), ((), ())), preferred_element_type=F32
    ).astype(BF)
    hid = grad.shape[1] // 2
    part = jnp.where(core_ref[0] == 0, grad[:, :hid].astype(F32), grad[:, hid:].astype(F32)).astype(BF)
    wgrad = lax.dot_general(agg, part, (((0,), (0,)), ((), ())), preferred_element_type=F32)

    @pl.when(b == 0)
    def _():
        wgrad_ref[...] = wgrad

    @pl.when(b > 0)
    def _():
        wgrad_ref[...] += wgrad

    width = own_ref.shape[3] // half
    k = b * (place_ref.shape[0] // rows)
    for ref in (own_ref, other_ref):
        for q in range(ref.shape[1]):
            term = lax.dot_general(
                ref[0, q], spread, (((0,), (0,)), ((), ())), preferred_element_type=F32
            ).astype(BF)
            for i in range(width):
                held[place_ref[k + i]] = term[i * half : (i + 1) * half]
            k += width

    @pl.when(b == rows - 1)
    def _():
        copies = []
        low = 0
        for i, out in enumerate(terms):
            size = out.shape[0]
            copies.append(pltpu.make_async_copy(held.at[pl.ds(low, size)], out, sems.at[i]))
            low += size
        for copy in copies:
            copy.start()
        for copy in copies:
            copy.wait()


def backward(core, place, mine, came, weight, cotangent, own, other, counts):
    rows, groups, side, wide = own.shape
    feat, hid = weight.shape
    tile_spec = pl.BlockSpec((1, groups, side, wide), lambda b: (b, 0, 0, 0))
    row_spec = pl.BlockSpec((1, side, feat), lambda b: (b, 0, 0))
    hid_spec = pl.BlockSpec((1, side, hid), lambda b: (b, 0, 0))
    smem = pl.BlockSpec(memory_space=pltpu.SMEM)
    return pl.pallas_call(
        backward_kernel,
        grid=(rows,),
        in_specs=[
            smem,
            smem,
            row_spec,
            row_spec,
            pl.BlockSpec((feat, hid), lambda b: (0, 0)),
            hid_spec,
            tile_spec,
            tile_spec,
        ],
        out_specs=[
            hid_spec,
            pl.BlockSpec((feat, hid // 2), lambda b: (0, 0)),
        ]
        + [pl.BlockSpec(memory_space=pl.ANY)] * len(counts),
        out_shape=[
            jax.ShapeDtypeStruct((rows, side, hid), BF),
            jax.ShapeDtypeStruct((feat, hid // 2), F32),
        ]
        + [jax.ShapeDtypeStruct((n, side // 2, feat), BF) for n in counts],
        scratch_shapes=[
            pltpu.VMEM((sum(counts), side // 2, feat), BF),
            pltpu.SemaphoreType.DMA((len(counts),)),
        ],
        compiler_params=pltpu.CompilerParams(vmem_limit_bytes=40 * 2**20),
        cost_estimate=pl.CostEstimate(flops=2**30, bytes_accessed=2**24, transcendentals=2**18),
        name="backward_tiles",
    )(core, place, mine, came, weight, cotangent, own, other)


def body(features, weight, tiles, tile_cols, order, cotangent):
    tile_rows, row_slots, side, _ = tiles.shape
    width = features.shape[1]
    n_tiles = order.shape[0]
    n_rows = lax.axis_size("rows")
    here = lax.axis_index("rows")
    core = lax.axis_index("rep")
    core_ref = core.reshape(1).astype(jnp.int32)
    half = side // 2
    group = 4 if row_slots % 4 == 0 else 2

    halves = features.reshape(tile_rows, 2, half, width)
    own_half = jnp.where(core == 0, halves[:, 0], halves[:, 1])
    labels = jnp.arange(n_tiles, dtype=jnp.int32)
    flat = tile_cols.reshape(-1)
    block = jnp.sum(jnp.where(flat[:, None] == labels[None, :], order[None, :], 0), axis=1)
    block = block.reshape(tile_rows, row_slots)
    first = late_sizes(n_rows)

    rounds = (((0, 1), (0, 1)),) * 4 + (
        ((1, 0), (1,)),
        ((1, 2), (0, 1, 2)),
        ((0, 1, 3), (0, 3)),
        ((0, 3), (0, 1, 3)),
        ((0, 1, 3), (0, 1, 3)),
    )
    single, pair = PARTS[0], PARTS[1:]
    chains = [
        gather_chain(n_rows, own_half[: single[1]], single[2]),
        gather_pair(n_rows, own_half[single[1] :], pair),
        index_chain(block),
        tile_chain(core_ref, tiles, group),
    ]
    pieces, pieces_pair, block, (own, other) = drive(chains, rounds if n_rows == 128 else ())
    pieces = pieces + pieces_pair[0] + pieces_pair[1]
    place = positions(n_rows, tile_rows, block, here, core)

    mine = forward(place, own, other, pieces)
    came = lax.ppermute(mine, "rep", SWAP)
    activated, wgrad, early, *late = backward(
        core_ref, arranged(n_rows, place, first), mine, came, weight,
        cotangent.reshape(tile_rows, side, -1), own, other, (n_tiles - sum(first),) + first,
    )

    every = (0, 1, 2)
    rounds = (
        (every, (2,)),
        ((2,), (0, 2)),
        ((0, 2), (2,)),
        ((2,), every),
        (every, every),
        (every, (1, 2)),
        ((1, 2), every),
    )
    buffers = []
    base = 0
    for (_, count, axes), out in zip(PARTS, late):
        size = count * n_rows - out.shape[0]
        buffers.append((early[base : base + size], out))
        base += size
    chains = [
        scatter_chain(n_rows, *buffers[0], single[2]),
        scatter_pair(n_rows, buffers[1:], pair),
        sum_chain(n_rows, wgrad),
    ]
    *owned, (wgrad, wother) = drive(chains, rounds if n_rows == 128 else ())
    weight_grad = jnp.where(
        core == 0, jnp.concatenate([wgrad, wother], 1), jnp.concatenate([wother, wgrad], 1)
    )
    owned = jnp.concatenate(owned, 0)
    across = lax.ppermute(owned, "rep", SWAP)
    feature_grad = jnp.where(
        core == 0, jnp.stack([owned, across], 1), jnp.stack([across, owned], 1)
    ).reshape(tile_rows * side, width)
    return activated.reshape(tile_rows * side, -1), feature_grad, weight_grad


def solution(mesh):
    in_specs = (
        P("rows", None),
        P(),
        P("rows", "rep", None, None),
        P("rows", "rep"),
        P(),
        P("rows", None),
    )
    out_specs = (P("rows", None), P("rows", None), P())
    return jax.shard_map(body, mesh=mesh, in_specs=in_specs, out_specs=out_specs, check_vma=False)
```

```python
import functools

import jax
import jax.numpy as jnp
from jax import lax
from jax.experimental import pallas as pl
from jax.experimental.pallas import tpu as pltpu
from jax.sharding import PartitionSpec as P

BF = jnp.bfloat16
F32 = jnp.float32
BOTH = ("rows", "rep")
SWAP = ((0, 1), (1, 0))


def torus(n_rows):
    return {128: (4, 8, 4), 8: (2, 2, 2)}[n_rows]


def swap(n_rows, axis, turn):
    sizes = torus(n_rows)
    pairs = []
    for i in range(n_rows):
        c = [i // (sizes[1] * sizes[2]), i // sizes[2] % sizes[1], i % sizes[2]]
        for core in range(2):
            t = list(c)
            t[axis] = (t[axis] + (1 if (t[axis] + core + turn) % 2 == 0 else -1)) % sizes[axis]
            pairs.append((2 * i + core, 2 * ((t[0] * sizes[1] + t[1]) * sizes[2] + t[2]) + core))
    return tuple(pairs)


PARTS = ((0, 2, (2, 0, 1)), (2, 3, (1, 0, 2)), (5, 3, (1, 2, 0)))
ARRIVAL = {2: (0, 1), 4: (0, 1, 3, 2), 8: (0, 1, 7, 6, 2, 3, 5, 4)}


def together(chains):
    asks = [next(c) for c in chains]
    results = [None] * len(chains)
    while any(ask is not None for ask in asks):
        came = yield [a for ask in asks if ask is not None for a in ask]
        for i, chain in enumerate(chains):
            if asks[i] is None:
                continue
            mine, came = came[: len(asks[i])], came[len(asks[i]) :]
            try:
                asks[i] = chain.send(mine)
            except StopIteration as stop:
                asks[i], results[i] = None, stop.value
    return results


def gather_pair(n_rows, own, parts):
    (_, count, (axis, *_)), (_, more, _) = parts
    held = yield from gather_chain(n_rows, own, (axis,), False)
    held = held.reshape((-1, count + more) + held.shape[1:])
    split = (held[:, :count], held[:, count:])
    split = [h.reshape((-1,) + own.shape[1:]) for h in split]
    chains = [gather_chain(n_rows, h, axes[1:]) for h, (_, _, axes) in zip(split, parts)]
    return (yield from together(chains))


def gather_chain(n_rows, own, axes, spread=True):
    sizes = torus(n_rows)
    held = own
    for axis in axes:
        n = sizes[axis]
        ahead, back = swap(n_rows, axis, 0), swap(n_rows, axis, 1)
        if spread and axis == axes[-1] and n == 4:
            one, two = yield [(held, BOTH, ahead), (held, BOTH, back)]
            (far,) = yield [(one, BOTH, back)]
            return [held, one, two, far]
        pieces = [held]
        send = held
        for step in range(n // 2):
            (got,) = yield [(send, BOTH, back if step % 2 else ahead)]
            pieces.append(got)
            send = jnp.concatenate([held, got], 0) if step == 0 else got
        if spread and axis == axes[-1]:
            return pieces
        held = lax.optimization_barrier(jnp.concatenate(pieces, 0))
    return held


def plus(a, b):
    return (a.astype(F32) + b.astype(F32)).astype(BF)


def scatter_pair(n_rows, buffers, parts):
    (_, count, (axis, *_)), (_, more, _) = parts
    chains = [
        scatter_chain(n_rows, early, late, axes[1:], False)
        for (early, late), (_, _, axes) in zip(buffers, parts)
    ]
    a, b = yield from together(chains)
    n = torus(n_rows)[axis]
    held = jnp.concatenate(
        [a.reshape((n, count) + a.shape[1:]), b.reshape((n, more) + b.shape[1:])], 1
    ).reshape((-1,) + a.shape[1:])
    cut = (count + more) * max(n - 2, 1)
    return (yield from scatter_chain(n_rows, held[:cut], held[cut:], (axis,)))


def scatter_chain(n_rows, early, late, axes, done=True):
    sizes = torus(n_rows)
    held = None
    for axis in axes[::-1]:
        n = sizes[axis]
        ahead, back = swap(n_rows, axis, 0), swap(n_rows, axis, 1)
        if held is not None:
            cut = held.shape[0] // n * max(n - 2, 1)
            early, late = held[:cut], held[cut:]
        size = (early.shape[0] + late.shape[0]) // n
        total = late
        first, second = early, late
        for step in range(n // 2 - 1, 0, -1):
            (got,) = yield [(total, BOTH, back if step % 2 else ahead)]
            kept = early[(2 * step - 2) * size : 2 * step * size]
            if step > 1:
                total = plus(got, kept)
            else:
                second = plus(got[size:], kept[size:])
                first = plus(got[:size], kept[:size])
        (got,) = yield [(second, BOTH, ahead)]
        held = first.astype(F32) + got.astype(F32)
        if axis != axes[0] or not done:
            held = held.astype(BF)
    return held


def index_chain(block):
    (got,) = yield [(block, "rep", SWAP)]
    return jnp.concatenate([block, got], 1).reshape(-1)


def tile_chain(core, tiles, group):
    (core,) = yield [core]
    own, send = pack(core, tiles, group)
    (send,) = yield [send]
    (other,) = yield [(send, "rep", SWAP)]
    return own, other


def sum_chain(n_rows, part):
    bit = 1
    while bit < n_rows:
        (got,) = yield [(part, "rows", tuple((i, i ^ bit) for i in range(n_rows)))]
        part = part + got
        bit *= 2
    (got,) = yield [(part, "rep", SWAP)]
    return part, got


def drive(chains, plan):
    asks = [next(c) for c in chains]
    flying = {}
    results = [None] * len(chains)

    def finish(names):
        names = [i for i in names if i in flying]
        if not names:
            return
        values = lax.optimization_barrier(tuple(tuple(flying.pop(i)) for i in names))
        for i, value in zip(names, values):
            try:
                asks[i] = chains[i].send(value)
            except StopIteration as stop:
                asks[i], results[i] = None, stop.value

    def start(names):
        for i in names:
            if asks[i] is not None and i not in flying:
                flying[i] = [lax.ppermute(*a) if isinstance(a, tuple) else a for a in asks[i]]

    for starts, ends in plan:
        start(starts)
        finish(ends)
    every = range(len(chains))
    while any(ask is not None for ask in asks):
        start(every)
        finish(every)
    return results


def late_sizes(n_rows):
    sizes = torus(n_rows)
    out = []
    for _, count, axes in PARTS:
        n = sizes[axes[-1]]
        out.append(count * n_rows // n * (1 if n == 2 else 2))
    return tuple(out)


def arranged(n_rows, place, late):
    base = 0
    tail = sum(count * n_rows for _, count, _ in PARTS) - sum(late)
    out = place
    for (first, count, _), last in zip(PARTS, late):
        early = count * n_rows - last
        inside = place - first * n_rows
        mine = (inside >= 0) & (inside < count * n_rows)
        at = jnp.where(inside < early, base + inside, tail + inside - early)
        out = jnp.where(mine, at, out)
        base += early
        tail += last
    return out


def positions(n_rows, tile_rows, block, here, core):
    sizes = torus(n_rows)
    owner, local = block // tile_rows, block % tile_rows

    def split(i):
        return (i // (sizes[1] * sizes[2]), i // sizes[2] % sizes[1], i % sizes[2])

    mine, theirs = split(here), split(owner)
    slot = []
    for axis in range(3):
        n = sizes[axis]
        turn = jnp.where((mine[axis] + core) % 2 == 0, 1, -1)
        offset = (turn * (theirs[axis] - mine[axis]) + n) % n
        slot.append(sum(jnp.where(offset == e, i, 0) for i, e in enumerate(ARRIVAL[n])))
    place = jnp.zeros_like(block)
    for first, count, axes in PARTS:
        a, b, c = axes
        at = ((slot[c] * sizes[b] + slot[b]) * sizes[a] + slot[a]) * count + local - first
        place = jnp.where((local >= first) & (local < first + count), first * n_rows + at, place)
    return place


def pack_kernel(width, core_ref, tiles_ref, own_ref, send_ref):
    side = tiles_ref.shape[2]
    half = side // 2

    def fill(first, second):
        for q in range(tiles_ref.shape[1] // width):
            group = [tiles_ref[0, q * width + i] for i in range(width)]
            first[0, q] = jnp.concatenate([t[:, :half] for t in group], 1)
            second[0, q] = jnp.concatenate([t[:, half:] for t in group], 1)

    @pl.when(core_ref[0] == 0)
    def _():
        fill(own_ref, send_ref)

    @pl.when(core_ref[0] != 0)
    def _():
        fill(send_ref, own_ref)


def pack(core, tiles, width):
    rows, slots, side, _ = tiles.shape
    packed = jax.ShapeDtypeStruct((rows, slots // width, side, width * side // 2), BF)
    spec = pl.BlockSpec((1, slots // width, side, width * side // 2), lambda b: (b, 0, 0, 0))
    return pl.pallas_call(
        functools.partial(pack_kernel, width),
        grid=(rows,),
        in_specs=[
            pl.BlockSpec(memory_space=pltpu.SMEM),
            pl.BlockSpec((1, slots, side, side), lambda b: (b, 0, 0, 0)),
        ],
        out_specs=[
            spec,
            spec,
        ],
        out_shape=[packed, packed],
        compiler_params=pltpu.CompilerParams(vmem_limit_bytes=40 * 2**20),
        cost_estimate=pl.CostEstimate(flops=0, bytes_accessed=2**24, transcendentals=0),
        name="pack_tiles",
    )(core, tiles)


def forward_kernel(place_ref, own_ref, other_ref, *refs):
    *pieces, sum_ref, held, sems = refs
    b = pl.program_id(0)
    half = held.shape[1]

    @pl.when(b == 0)
    def _():
        copies = []
        low = 0
        for i, piece in enumerate(pieces):
            size = piece.shape[0]
            copies.append(pltpu.make_async_copy(piece, held.at[pl.ds(low, size)], sems.at[i]))
            low += size
        for copy in copies:
            copy.start()
        for copy in copies:
            copy.wait()

    total = jnp.zeros(sum_ref.shape[1:], F32)
    width = own_ref.shape[3] // half
    k = b * (place_ref.shape[0] // pl.num_programs(0))
    for ref in (own_ref, other_ref):
        for q in range(ref.shape[1]):
            right = jnp.concatenate([held[place_ref[k + i]] for i in range(width)], 0)
            total += jnp.dot(ref[0, q], right, preferred_element_type=F32)
            k += width
    sum_ref[0] = total


def forward(place, own, other, pieces):
    rows, groups, side, wide = own.shape
    n_tiles = sum(p.shape[0] for p in pieces)
    half, width = pieces[0].shape[1:]
    spec = pl.BlockSpec((1, groups, side, wide), lambda b: (b, 0, 0, 0))
    return pl.pallas_call(
        forward_kernel,
        grid=(rows,),
        in_specs=[pl.BlockSpec(memory_space=pltpu.SMEM), spec, spec]
        + [pl.BlockSpec(memory_space=pl.ANY)] * len(pieces),
        out_specs=pl.BlockSpec((1, side, width), lambda b: (b, 0, 0)),
        out_shape=jax.ShapeDtypeStruct((rows, side, width), F32),
        scratch_shapes=[
            pltpu.VMEM((n_tiles, half, width), BF),
            pltpu.SemaphoreType.DMA((len(pieces),)),
        ],
        compiler_params=pltpu.CompilerParams(vmem_limit_bytes=58 * 2**20),
        cost_estimate=pl.CostEstimate(flops=2**30, bytes_accessed=3 * 2**23, transcendentals=0),
        name="forward_tiles",
    )(place, own, other, *pieces)


def backward_kernel(
    core_ref, place_ref, mine_ref, came_ref, weight_ref, cot_ref, own_ref, other_ref, *refs
):
    act_ref, wgrad_ref, *terms, held, sems = refs
    b = pl.program_id(0)
    rows = pl.num_programs(0)
    half = held.shape[1]

    @pl.when(b == 0)
    def _():
        @pl.loop(0, held.shape[0] // 8)
        def _(i):
            held[pl.ds(i * 8, 8)] = jnp.zeros((8,) + held.shape[1:], BF)

    agg = (mine_ref[0] + came_ref[0]).astype(BF)
    weight = weight_ref[...]
    pre = jnp.dot(agg, weight, preferred_element_type=F32)
    sig = jax.nn.sigmoid(pre)
    act_ref[0] = (pre * sig).astype(BF)
    grad = (cot_ref[0].astype(F32) * sig * (1.0 + pre * (1.0 - sig))).astype(BF)
    spread = lax.dot_general(
        grad, weight, (((1,), (1,)), ((), ())), preferred_element_type=F32
    ).astype(BF)
    hid = grad.shape[1] // 2
    part = jnp.where(core_ref[0] == 0, grad[:, :hid].astype(F32), grad[:, hid:].astype(F32)).astype(BF)
    wgrad = lax.dot_general(agg, part, (((0,), (0,)), ((), ())), preferred_element_type=F32)

    @pl.when(b == 0)
    def _():
        wgrad_ref[...] = wgrad

    @pl.when(b > 0)
    def _():
        wgrad_ref[...] += wgrad

    width = own_ref.shape[3] // half
    k = b * (place_ref.shape[0] // rows)
    for ref in (own_ref, other_ref):
        for q in range(ref.shape[1]):
            term = lax.dot_general(
                ref[0, q], spread, (((0,), (0,)), ((), ())), preferred_element_type=F32
            ).astype(BF)
            for i in range(width):
                held[place_ref[k + i]] = term[i * half : (i + 1) * half]
            k += width

    @pl.when(b == rows - 1)
    def _():
        copies = []
        low = 0
        for i, out in enumerate(terms):
            size = out.shape[0]
            copies.append(pltpu.make_async_copy(held.at[pl.ds(low, size)], out, sems.at[i]))
            low += size
        for copy in copies:
            copy.start()
        for copy in copies:
            copy.wait()


def backward(core, place, mine, came, weight, cotangent, own, other, counts):
    rows, groups, side, wide = own.shape
    feat, hid = weight.shape
    tile_spec = pl.BlockSpec((1, groups, side, wide), lambda b: (b, 0, 0, 0))
    row_spec = pl.BlockSpec((1, side, feat), lambda b: (b, 0, 0))
    hid_spec = pl.BlockSpec((1, side, hid), lambda b: (b, 0, 0))
    smem = pl.BlockSpec(memory_space=pltpu.SMEM)
    return pl.pallas_call(
        backward_kernel,
        grid=(rows,),
        in_specs=[
            smem,
            smem,
            row_spec,
            row_spec,
            pl.BlockSpec((feat, hid), lambda b: (0, 0)),
            hid_spec,
            tile_spec,
            tile_spec,
        ],
        out_specs=[
            hid_spec,
            pl.BlockSpec((feat, hid // 2), lambda b: (0, 0)),
        ]
        + [pl.BlockSpec(memory_space=pl.ANY)] * len(counts),
        out_shape=[
            jax.ShapeDtypeStruct((rows, side, hid), BF),
            jax.ShapeDtypeStruct((feat, hid // 2), F32),
        ]
        + [jax.ShapeDtypeStruct((n, side // 2, feat), BF) for n in counts],
        scratch_shapes=[
            pltpu.VMEM((sum(counts), side // 2, feat), BF),
            pltpu.SemaphoreType.DMA((len(counts),)),
        ],
        compiler_params=pltpu.CompilerParams(vmem_limit_bytes=58 * 2**20),
        cost_estimate=pl.CostEstimate(flops=2**30, bytes_accessed=2**24, transcendentals=2**18),
        name="backward_tiles",
    )(core, place, mine, came, weight, cotangent, own, other)


def body(features, weight, tiles, tile_cols, order, cotangent):
    tile_rows, row_slots, side, _ = tiles.shape
    width = features.shape[1]
    n_tiles = order.shape[0]
    n_rows = lax.axis_size("rows")
    here = lax.axis_index("rows")
    core = lax.axis_index("rep")
    core_ref = core.reshape(1).astype(jnp.int32)
    half = side // 2
    group = 4 if row_slots % 4 == 0 else 2

    halves = features.reshape(tile_rows, 2, half, width)
    own_half = jnp.where(core == 0, halves[:, 0], halves[:, 1])
    labels = jnp.arange(n_tiles, dtype=jnp.int32)
    flat = tile_cols.reshape(-1)
    block = jnp.sum(jnp.where(flat[:, None] == labels[None, :], order[None, :], 0), axis=1)
    block = block.reshape(tile_rows, row_slots)
    first = late_sizes(n_rows)

    rounds = (((0, 1), (0, 1)),) * 4 + (
        ((1, 0), (1,)),
        ((1, 2), (0, 1, 2)),
        ((0, 1, 3), (0, 3)),
        ((0, 3), (0, 1, 3)),
        ((0, 1, 3), (0, 1, 3)),
    )
    single, pair = PARTS[0], PARTS[1:]
    chains = [
        gather_chain(n_rows, own_half[: single[1]], single[2]),
        gather_pair(n_rows, own_half[single[1] :], pair),
        index_chain(block),
        tile_chain(core_ref, tiles, group),
    ]
    pieces, pieces_pair, block, (own, other) = drive(chains, rounds if n_rows == 128 else ())
    pieces = pieces + pieces_pair[0] + pieces_pair[1]
    place = positions(n_rows, tile_rows, block, here, core)

    mine = forward(place, own, other, pieces)
    came = lax.ppermute(mine, "rep", SWAP)
    activated, wgrad, early, *late = backward(
        core_ref, arranged(n_rows, place, first), mine, came, weight,
        cotangent.reshape(tile_rows, side, -1), own, other, (n_tiles - sum(first),) + first,
    )

    every = (0, 1, 2)
    rounds = (
        (every, (0,)),
        ((0,), every),
        (every, every),
        (every, (1, 2)),
        ((1, 2), every),
    )
    buffers = []
    base = 0
    for (_, count, axes), out in zip(PARTS, late):
        size = count * n_rows - out.shape[0]
        buffers.append((early[base : base + size], out))
        base += size
    chains = [
        scatter_chain(n_rows, *buffers[0], single[2]),
        scatter_pair(n_rows, buffers[1:], pair),
        sum_chain(n_rows, wgrad),
    ]
    *owned, (wgrad, wother) = drive(chains, rounds if n_rows == 128 else ())
    weight_grad = jnp.where(
        core == 0, jnp.concatenate([wgrad, wother], 1), jnp.concatenate([wother, wgrad], 1)
    )
    owned = jnp.concatenate(owned, 0)
    across = lax.ppermute(owned, "rep", SWAP)
    feature_grad = jnp.where(
        core == 0, jnp.stack([owned, across], 1), jnp.stack([across, owned], 1)
    ).reshape(tile_rows * side, width)
    return activated.reshape(tile_rows * side, -1), feature_grad, weight_grad


def solution(mesh):
    in_specs = (
        P("rows", None),
        P(),
        P("rows", "rep", None, None),
        P("rows", "rep"),
        P(),
        P("rows", None),
    )
    out_specs = (P("rows", None), P("rows", None), P())
    return jax.shard_map(body, mesh=mesh, in_specs=in_specs, out_specs=out_specs, check_vma=False)
```

```python
import functools

import jax
import jax.numpy as jnp
from jax import lax
from jax.experimental import pallas as pl
from jax.experimental.pallas import tpu as pltpu
from jax.sharding import PartitionSpec as P

BF = jnp.bfloat16
F32 = jnp.float32
BOTH = ("rows", "rep")
SWAP = ((0, 1), (1, 0))


def torus(n_rows):
    return {128: (4, 8, 4), 8: (2, 2, 2)}[n_rows]


def swap(n_rows, axis, turn):
    sizes = torus(n_rows)
    pairs = []
    for i in range(n_rows):
        c = [i // (sizes[1] * sizes[2]), i // sizes[2] % sizes[1], i % sizes[2]]
        for core in range(2):
            t = list(c)
            t[axis] = (t[axis] + (1 if (t[axis] + core + turn) % 2 == 0 else -1)) % sizes[axis]
            pairs.append((2 * i + core, 2 * ((t[0] * sizes[1] + t[1]) * sizes[2] + t[2]) + core))
    return tuple(pairs)


PARTS = ((0, 2, (2, 0, 1)), (2, 3, (1, 0, 2)), (5, 3, (1, 2, 0)))
ARRIVAL = {2: (0, 1), 4: (0, 1, 3, 2), 8: (0, 1, 7, 6, 2, 3, 5, 4)}


def together(chains):
    asks = [next(c) for c in chains]
    results = [None] * len(chains)
    while any(ask is not None for ask in asks):
        came = yield [a for ask in asks if ask is not None for a in ask]
        for i, chain in enumerate(chains):
            if asks[i] is None:
                continue
            mine, came = came[: len(asks[i])], came[len(asks[i]) :]
            try:
                asks[i] = chain.send(mine)
            except StopIteration as stop:
                asks[i], results[i] = None, stop.value
    return results


def gather_pair(n_rows, own, parts):
    (_, count, (axis, *_)), (_, more, _) = parts
    held = yield from gather_chain(n_rows, own, (axis,), False)
    held = held.reshape((-1, count + more) + held.shape[1:])
    split = (held[:, :count], held[:, count:])
    split = [h.reshape((-1,) + own.shape[1:]) for h in split]
    chains = [gather_chain(n_rows, h, axes[1:]) for h, (_, _, axes) in zip(split, parts)]
    return (yield from together(chains))


def gather_chain(n_rows, own, axes, spread=True):
    sizes = torus(n_rows)
    held = own
    for axis in axes:
        n = sizes[axis]
        ahead, back = swap(n_rows, axis, 0), swap(n_rows, axis, 1)
        if spread and axis == axes[-1] and n == 4:
            one, two = yield [(held, BOTH, ahead), (held, BOTH, back)]
            (far,) = yield [(one, BOTH, back)]
            return [held, one, two, far]
        pieces = [held]
        send = held
        for step in range(n // 2):
            (got,) = yield [(send, BOTH, back if step % 2 else ahead)]
            pieces.append(got)
            send = jnp.concatenate([held, got], 0) if step == 0 else got
        if spread and axis == axes[-1]:
            return pieces
        held = lax.optimization_barrier(jnp.concatenate(pieces, 0))
    return held


def plus(a, b):
    return (a.astype(F32) + b.astype(F32)).astype(BF)


def scatter_pair(n_rows, buffers, parts):
    (_, count, (axis, *_)), (_, more, _) = parts
    chains = [
        scatter_chain(n_rows, early, late, axes[1:], False)
        for (early, late), (_, _, axes) in zip(buffers, parts)
    ]
    a, b = yield from together(chains)
    n = torus(n_rows)[axis]
    held = jnp.concatenate(
        [a.reshape((n, count) + a.shape[1:]), b.reshape((n, more) + b.shape[1:])], 1
    ).reshape((-1,) + a.shape[1:])
    cut = (count + more) * max(n - 2, 1)
    return (yield from scatter_chain(n_rows, held[:cut], held[cut:], (axis,)))


def scatter_chain(n_rows, early, late, axes, done=True):
    sizes = torus(n_rows)
    held = None
    for axis in axes[::-1]:
        n = sizes[axis]
        ahead, back = swap(n_rows, axis, 0), swap(n_rows, axis, 1)
        if held is not None:
            cut = held.shape[0] // n * max(n - 2, 1)
            early, late = held[:cut], held[cut:]
        size = (early.shape[0] + late.shape[0]) // n
        total = late
        first, second = early, late
        for step in range(n // 2 - 1, 0, -1):
            (got,) = yield [(total, BOTH, back if step % 2 else ahead)]
            kept = early[(2 * step - 2) * size : 2 * step * size]
            if step > 1:
                total = plus(got, kept)
            else:
                second = plus(got[size:], kept[size:])
                first = plus(got[:size], kept[:size])
        (got,) = yield [(second, BOTH, ahead)]
        held = first.astype(F32) + got.astype(F32)
        if axis != axes[0] or not done:
            held = held.astype(BF)
    return held


def index_chain(block):
    (got,) = yield [(block, "rep", SWAP)]
    return jnp.concatenate([block, got], 1).reshape(-1)


def tile_chain(core, tiles, group):
    (core,) = yield [core]
    own, send = pack(core, tiles, group)
    (send,) = yield [send]
    (other,) = yield [(send, "rep", SWAP)]
    return own, other


def sum_chain(n_rows, part):
    bit = 1
    while bit < n_rows:
        (got,) = yield [(part, "rows", tuple((i, i ^ bit) for i in range(n_rows)))]
        part = part + got
        bit *= 2
    return part


def drive(chains, plan):
    asks = [next(c) for c in chains]
    flying = {}
    results = [None] * len(chains)

    def finish(names):
        names = [i for i in names if i in flying]
        if not names:
            return
        values = lax.optimization_barrier(tuple(tuple(flying.pop(i)) for i in names))
        for i, value in zip(names, values):
            try:
                asks[i] = chains[i].send(value)
            except StopIteration as stop:
                asks[i], results[i] = None, stop.value

    def start(names):
        for i in names:
            if asks[i] is not None and i not in flying:
                flying[i] = [lax.ppermute(*a) if isinstance(a, tuple) else a for a in asks[i]]

    for starts, ends in plan:
        start(starts)
        finish(ends)
    every = range(len(chains))
    while any(ask is not None for ask in asks):
        start(every)
        finish(every)
    return results


def late_sizes(n_rows):
    sizes = torus(n_rows)
    out = []
    for _, count, axes in PARTS:
        n = sizes[axes[-1]]
        out.append(count * n_rows // n * (1 if n == 2 else 2))
    return tuple(out)


def arranged(n_rows, place, late):
    base = 0
    tail = sum(count * n_rows for _, count, _ in PARTS) - sum(late)
    out = place
    for (first, count, _), last in zip(PARTS, late):
        early = count * n_rows - last
        inside = place - first * n_rows
        mine = (inside >= 0) & (inside < count * n_rows)
        at = jnp.where(inside < early, base + inside, tail + inside - early)
        out = jnp.where(mine, at, out)
        base += early
        tail += last
    return out


def positions(n_rows, tile_rows, block, here, core):
    sizes = torus(n_rows)
    owner, local = block // tile_rows, block % tile_rows

    def split(i):
        return (i // (sizes[1] * sizes[2]), i // sizes[2] % sizes[1], i % sizes[2])

    mine, theirs = split(here), split(owner)
    slot = []
    for axis in range(3):
        n = sizes[axis]
        turn = jnp.where((mine[axis] + core) % 2 == 0, 1, -1)
        offset = (turn * (theirs[axis] - mine[axis]) + n) % n
        slot.append(sum(jnp.where(offset == e, i, 0) for i, e in enumerate(ARRIVAL[n])))
    place = jnp.zeros_like(block)
    for first, count, axes in PARTS:
        a, b, c = axes
        at = ((slot[c] * sizes[b] + slot[b]) * sizes[a] + slot[a]) * count + local - first
        place = jnp.where((local >= first) & (local < first + count), first * n_rows + at, place)
    return place


def pack_kernel(width, core_ref, tiles_ref, own_ref, send_ref):
    side = tiles_ref.shape[2]
    half = side // 2

    def fill(first, second):
        for q in range(tiles_ref.shape[1] // width):
            group = [tiles_ref[0, q * width + i] for i in range(width)]
            first[0, q] = jnp.concatenate([t[:, :half] for t in group], 1)
            second[0, q] = jnp.concatenate([t[:, half:] for t in group], 1)

    @pl.when(core_ref[0] == 0)
    def _():
        fill(own_ref, send_ref)

    @pl.when(core_ref[0] != 0)
    def _():
        fill(send_ref, own_ref)


def pack(core, tiles, width):
    rows, slots, side, _ = tiles.shape
    packed = jax.ShapeDtypeStruct((rows, slots // width, side, width * side // 2), BF)
    spec = pl.BlockSpec((1, slots // width, side, width * side // 2), lambda b: (b, 0, 0, 0))
    return pl.pallas_call(
        functools.partial(pack_kernel, width),
        grid=(rows,),
        in_specs=[
            pl.BlockSpec(memory_space=pltpu.SMEM),
            pl.BlockSpec((1, slots, side, side), lambda b: (b, 0, 0, 0)),
        ],
        out_specs=[
            spec,
            spec,
        ],
        out_shape=[packed, packed],
        compiler_params=pltpu.CompilerParams(vmem_limit_bytes=40 * 2**20),
        cost_estimate=pl.CostEstimate(flops=0, bytes_accessed=2**24, transcendentals=0),
        name="pack_tiles",
    )(core, tiles)


def forward_kernel(place_ref, own_ref, other_ref, *refs):
    *pieces, sum_ref, held, sems = refs
    b = pl.program_id(0)
    half = held.shape[1]

    @pl.when(b == 0)
    def _():
        copies = []
        low = 0
        for i, piece in enumerate(pieces):
            size = piece.shape[0]
            copies.append(pltpu.make_async_copy(piece, held.at[pl.ds(low, size)], sems.at[i]))
            low += size
        for copy in copies:
            copy.start()
        for copy in copies:
            copy.wait()

    total = jnp.zeros(sum_ref.shape[1:], F32)
    width = own_ref.shape[3] // half
    k = b * (place_ref.shape[0] // pl.num_programs(0))
    for ref in (own_ref, other_ref):
        for q in range(ref.shape[1]):
            right = jnp.concatenate([held[place_ref[k + i]] for i in range(width)], 0)
            total += jnp.dot(ref[0, q], right, preferred_element_type=F32)
            k += width
    sum_ref[0] = total


def forward(place, own, other, pieces):
    rows, groups, side, wide = own.shape
    n_tiles = sum(p.shape[0] for p in pieces)
    half, width = pieces[0].shape[1:]
    spec = pl.BlockSpec((1, groups, side, wide), lambda b: (b, 0, 0, 0))
    return pl.pallas_call(
        forward_kernel,
        grid=(rows,),
        in_specs=[pl.BlockSpec(memory_space=pltpu.SMEM), spec, spec]
        + [pl.BlockSpec(memory_space=pl.ANY)] * len(pieces),
        out_specs=pl.BlockSpec((1, side, width), lambda b: (b, 0, 0)),
        out_shape=jax.ShapeDtypeStruct((rows, side, width), F32),
        scratch_shapes=[
            pltpu.VMEM((n_tiles, half, width), BF),
            pltpu.SemaphoreType.DMA((len(pieces),)),
        ],
        compiler_params=pltpu.CompilerParams(vmem_limit_bytes=58 * 2**20),
        cost_estimate=pl.CostEstimate(flops=2**30, bytes_accessed=3 * 2**23, transcendentals=0),
        name="forward_tiles",
    )(place, own, other, *pieces)


def backward_kernel(
    core_ref, place_ref, mine_ref, came_ref, weight_ref, cot_ref, own_ref, other_ref, *refs
):
    act_ref, wgrad_ref, *terms, held, sems = refs
    b = pl.program_id(0)
    rows = pl.num_programs(0)
    half = held.shape[1]

    @pl.when(b == 0)
    def _():
        @pl.loop(0, held.shape[0] // 8)
        def _(i):
            held[pl.ds(i * 8, 8)] = jnp.zeros((8,) + held.shape[1:], BF)

    agg = (mine_ref[0] + came_ref[0]).astype(BF)
    weight = weight_ref[...]
    pre = jnp.dot(agg, weight, preferred_element_type=F32)
    sig = jax.nn.sigmoid(pre)
    act_ref[0] = (pre * sig).astype(BF)
    grad = (cot_ref[0].astype(F32) * sig * (1.0 + pre * (1.0 - sig))).astype(BF)
    spread = lax.dot_general(
        grad, weight, (((1,), (1,)), ((), ())), preferred_element_type=F32
    ).astype(BF)
    hid = grad.shape[1] // 2
    part = jnp.where(core_ref[0] == 0, grad[:, :hid].astype(F32), grad[:, hid:].astype(F32)).astype(BF)
    wgrad = lax.dot_general(agg, part, (((0,), (0,)), ((), ())), preferred_element_type=F32)

    @pl.when(b == 0)
    def _():
        wgrad_ref[...] = wgrad

    @pl.when(b > 0)
    def _():
        wgrad_ref[...] += wgrad

    width = own_ref.shape[3] // half
    k = b * (place_ref.shape[0] // rows)
    for ref in (own_ref, other_ref):
        for q in range(ref.shape[1]):
            term = lax.dot_general(
                ref[0, q], spread, (((0,), (0,)), ((), ())), preferred_element_type=F32
            ).astype(BF)
            for i in range(width):
                held[place_ref[k + i]] = term[i * half : (i + 1) * half]
            k += width

    @pl.when(b == rows - 1)
    def _():
        copies = []
        low = 0
        for i, out in enumerate(terms):
            size = out.shape[0]
            copies.append(pltpu.make_async_copy(held.at[pl.ds(low, size)], out, sems.at[i]))
            low += size
        for copy in copies:
            copy.start()
        for copy in copies:
            copy.wait()


def backward(core, place, mine, came, weight, cotangent, own, other, counts):
    rows, groups, side, wide = own.shape
    feat, hid = weight.shape
    tile_spec = pl.BlockSpec((1, groups, side, wide), lambda b: (b, 0, 0, 0))
    row_spec = pl.BlockSpec((1, side, feat), lambda b: (b, 0, 0))
    hid_spec = pl.BlockSpec((1, side, hid), lambda b: (b, 0, 0))
    smem = pl.BlockSpec(memory_space=pltpu.SMEM)
    return pl.pallas_call(
        backward_kernel,
        grid=(rows,),
        in_specs=[
            smem,
            smem,
            row_spec,
            row_spec,
            pl.BlockSpec((feat, hid), lambda b: (0, 0)),
            hid_spec,
            tile_spec,
            tile_spec,
        ],
        out_specs=[
            hid_spec,
            pl.BlockSpec((feat, hid // 2), lambda b: (0, 0)),
        ]
        + [pl.BlockSpec(memory_space=pl.ANY)] * len(counts),
        out_shape=[
            jax.ShapeDtypeStruct((rows, side, hid), BF),
            jax.ShapeDtypeStruct((feat, hid // 2), F32),
        ]
        + [jax.ShapeDtypeStruct((n, side // 2, feat), BF) for n in counts],
        scratch_shapes=[
            pltpu.VMEM((sum(counts), side // 2, feat), BF),
            pltpu.SemaphoreType.DMA((len(counts),)),
        ],
        compiler_params=pltpu.CompilerParams(vmem_limit_bytes=40 * 2**20),
        cost_estimate=pl.CostEstimate(flops=2**30, bytes_accessed=2**24, transcendentals=2**18),
        name="backward_tiles",
    )(core, place, mine, came, weight, cotangent, own, other)


def body(features, weight, tiles, tile_cols, order, cotangent):
    tile_rows, row_slots, side, _ = tiles.shape
    width = features.shape[1]
    n_tiles = order.shape[0]
    n_rows = lax.axis_size("rows")
    here = lax.axis_index("rows")
    core = lax.axis_index("rep")
    core_ref = core.reshape(1).astype(jnp.int32)
    half = side // 2
    group = 4 if row_slots % 4 == 0 else 2

    halves = features.reshape(tile_rows, 2, half, width)
    own_half = jnp.where(core == 0, halves[:, 0], halves[:, 1])
    labels = jnp.arange(n_tiles, dtype=jnp.int32)
    flat = tile_cols.reshape(-1)
    block = jnp.sum(jnp.where(flat[:, None] == labels[None, :], order[None, :], 0), axis=1)
    block = block.reshape(tile_rows, row_slots)
    first = late_sizes(n_rows)

    rounds = (((0, 1), (0, 1)),) * 4 + (
        ((1, 0), (1,)),
        ((1, 2), (0, 1, 2)),
        ((0, 1, 3), (0, 3)),
        ((0, 3), (0, 1, 3)),
        ((0, 1, 3), (0, 1, 3)),
    )
    single, pair = PARTS[0], PARTS[1:]
    chains = [
        gather_chain(n_rows, own_half[: single[1]], single[2]),
        gather_pair(n_rows, own_half[single[1] :], pair),
        index_chain(block),
        tile_chain(core_ref, tiles, group),
    ]
    pieces, pieces_pair, block, (own, other) = drive(chains, rounds if n_rows == 128 else ())
    pieces = pieces + pieces_pair[0] + pieces_pair[1]
    place = positions(n_rows, tile_rows, block, here, core)

    mine = forward(place, own, other, pieces)
    came = lax.ppermute(mine, "rep", SWAP)
    activated, wgrad, early, *late = backward(
        core_ref, arranged(n_rows, place, first), mine, came, weight,
        cotangent.reshape(tile_rows, side, -1), own, other, (n_tiles - sum(first),) + first,
    )

    every = (0, 1, 2)
    rounds = (
        (every, (0,)),
        ((0,), every),
        (every, every),
        (every, (1, 2)),
        ((1, 2), every),
    )
    buffers = []
    base = 0
    for (_, count, axes), out in zip(PARTS, late):
        size = count * n_rows - out.shape[0]
        buffers.append((early[base : base + size], out))
        base += size
    chains = [
        scatter_chain(n_rows, *buffers[0], single[2]),
        scatter_pair(n_rows, buffers[1:], pair),
        sum_chain(n_rows, wgrad),
    ]
    *owned, wgrad = drive(chains, rounds if n_rows == 128 else ())
    owned, wgrad = lax.optimization_barrier((jnp.concatenate(owned, 0), wgrad))
    wother = lax.ppermute(wgrad, "rep", SWAP)
    weight_grad = jnp.where(
        core == 0, jnp.concatenate([wgrad, wother], 1), jnp.concatenate([wother, wgrad], 1)
    )
    across = lax.ppermute(owned, "rep", SWAP)
    feature_grad = jnp.where(
        core == 0, jnp.stack([owned, across], 1), jnp.stack([across, owned], 1)
    ).reshape(tile_rows * side, width)
    return activated.reshape(tile_rows * side, -1), feature_grad, weight_grad


def solution(mesh):
    in_specs = (
        P("rows", None),
        P(),
        P("rows", "rep", None, None),
        P("rows", "rep"),
        P(),
        P("rows", None),
    )
    out_specs = (P("rows", None), P("rows", None), P())
    return jax.shard_map(body, mesh=mesh, in_specs=in_specs, out_specs=out_specs, check_vma=False)
```

```python
import functools

import jax
import jax.numpy as jnp
from jax import lax
from jax.experimental import pallas as pl
from jax.experimental.pallas import tpu as pltpu
from jax.sharding import PartitionSpec as P

BF = jnp.bfloat16
F32 = jnp.float32
BOTH = ("rows", "rep")
SWAP = ((0, 1), (1, 0))


def torus(n_rows):
    return {128: (4, 8, 4), 8: (2, 2, 2)}[n_rows]


def swap(n_rows, axis, turn):
    sizes = torus(n_rows)
    pairs = []
    for i in range(n_rows):
        c = [i // (sizes[1] * sizes[2]), i // sizes[2] % sizes[1], i % sizes[2]]
        for core in range(2):
            t = list(c)
            t[axis] = (t[axis] + (1 if (t[axis] + core + turn) % 2 == 0 else -1)) % sizes[axis]
            pairs.append((2 * i + core, 2 * ((t[0] * sizes[1] + t[1]) * sizes[2] + t[2]) + core))
    return tuple(pairs)


PARTS = ((0, 2, (2, 0, 1)), (2, 3, (1, 0, 2)), (5, 3, (1, 2, 0)))
ARRIVAL = {2: (0, 1), 4: (0, 1, 3, 2), 8: (0, 1, 7, 6, 2, 3, 5, 4)}


def together(chains):
    asks = [next(c) for c in chains]
    results = [None] * len(chains)
    while any(ask is not None for ask in asks):
        came = yield [a for ask in asks if ask is not None for a in ask]
        for i, chain in enumerate(chains):
            if asks[i] is None:
                continue
            mine, came = came[: len(asks[i])], came[len(asks[i]) :]
            try:
                asks[i] = chain.send(mine)
            except StopIteration as stop:
                asks[i], results[i] = None, stop.value
    return results


def gather_pair(n_rows, own, parts):
    (_, count, (axis, *_)), (_, more, _) = parts
    held = yield from gather_chain(n_rows, own, (axis,), False)
    held = held.reshape((-1, count + more) + held.shape[1:])
    split = (held[:, :count], held[:, count:])
    split = [h.reshape((-1,) + own.shape[1:]) for h in split]
    chains = [gather_chain(n_rows, h, axes[1:]) for h, (_, _, axes) in zip(split, parts)]
    return (yield from together(chains))


def gather_chain(n_rows, own, axes, spread=True):
    sizes = torus(n_rows)
    held = own
    for axis in axes:
        n = sizes[axis]
        ahead, back = swap(n_rows, axis, 0), swap(n_rows, axis, 1)
        if spread and axis == axes[-1] and n == 4:
            one, two = yield [(held, BOTH, ahead), (held, BOTH, back)]
            (far,) = yield [(one, BOTH, back)]
            return [held, one, two, far]
        pieces = [held]
        send = held
        for step in range(n // 2):
            (got,) = yield [(send, BOTH, back if step % 2 else ahead)]
            pieces.append(got)
            send = jnp.concatenate([held, got], 0) if step == 0 else got
        if spread and axis == axes[-1]:
            return pieces
        held = lax.optimization_barrier(jnp.concatenate(pieces, 0))
    return held


def plus(a, b):
    return (a.astype(F32) + b.astype(F32)).astype(BF)


def scatter_pair(n_rows, buffers, parts):
    (_, count, (axis, *_)), (_, more, _) = parts
    chains = [
        scatter_chain(n_rows, early, late, axes[1:], False)
        for (early, late), (_, _, axes) in zip(buffers, parts)
    ]
    a, b = yield from together(chains)
    n = torus(n_rows)[axis]
    held = jnp.concatenate(
        [a.reshape((n, count) + a.shape[1:]), b.reshape((n, more) + b.shape[1:])], 1
    ).reshape((-1,) + a.shape[1:])
    cut = (count + more) * max(n - 2, 1)
    return (yield from scatter_chain(n_rows, held[:cut], held[cut:], (axis,)))


def scatter_chain(n_rows, early, late, axes, done=True):
    sizes = torus(n_rows)
    held = None
    for axis in axes[::-1]:
        n = sizes[axis]
        ahead, back = swap(n_rows, axis, 0), swap(n_rows, axis, 1)
        if held is not None:
            cut = held.shape[0] // n * max(n - 2, 1)
            early, late = held[:cut], held[cut:]
        size = (early.shape[0] + late.shape[0]) // n
        total = late
        first, second = early, late
        for step in range(n // 2 - 1, 0, -1):
            (got,) = yield [(total, BOTH, back if step % 2 else ahead)]
            kept = early[(2 * step - 2) * size : 2 * step * size]
            if step > 1:
                total = plus(got, kept)
            else:
                second = plus(got[size:], kept[size:])
                first = plus(got[:size], kept[:size])
        (got,) = yield [(second, BOTH, ahead)]
        held = first.astype(F32) + got.astype(F32)
        if axis != axes[0] or not done:
            held = held.astype(BF)
    return held


def index_chain(block):
    (got,) = yield [(block, "rep", SWAP)]
    return jnp.concatenate([block, got], 1).reshape(-1)


def tile_chain(core, tiles, group):
    (core,) = yield [core]
    own, send = pack(core, tiles, group)
    (send,) = yield [send]
    (other,) = yield [(send, "rep", SWAP)]
    return own, other


def sum_chain(n_rows, part):
    bit = 1
    while bit < n_rows:
        (got,) = yield [(part, "rows", tuple((i, i ^ bit) for i in range(n_rows)))]
        part = part + got
        bit *= 2
    return part


def drive(chains, plan):
    asks = [next(c) for c in chains]
    flying = {}
    results = [None] * len(chains)

    def finish(names):
        names = [i for i in names if i in flying]
        if not names:
            return
        values = lax.optimization_barrier(tuple(tuple(flying.pop(i)) for i in names))
        for i, value in zip(names, values):
            try:
                asks[i] = chains[i].send(value)
            except StopIteration as stop:
                asks[i], results[i] = None, stop.value

    def start(names):
        for i in names:
            if asks[i] is not None and i not in flying:
                flying[i] = [lax.ppermute(*a) if isinstance(a, tuple) else a for a in asks[i]]

    for starts, ends in plan:
        start(starts)
        finish(ends)
    every = range(len(chains))
    while any(ask is not None for ask in asks):
        start(every)
        finish(every)
    return results


def late_sizes(n_rows):
    sizes = torus(n_rows)
    out = []
    for _, count, axes in PARTS:
        n = sizes[axes[-1]]
        out.append(count * n_rows // n * (1 if n == 2 else 2))
    return tuple(out)


def arranged(n_rows, place, late):
    base = 0
    tail = sum(count * n_rows for _, count, _ in PARTS) - sum(late)
    out = place
    for (first, count, _), last in zip(PARTS, late):
        early = count * n_rows - last
        inside = place - first * n_rows
        mine = (inside >= 0) & (inside < count * n_rows)
        at = jnp.where(inside < early, base + inside, tail + inside - early)
        out = jnp.where(mine, at, out)
        base += early
        tail += last
    return out


def positions(n_rows, tile_rows, block, here, core):
    sizes = torus(n_rows)
    owner, local = block // tile_rows, block % tile_rows

    def split(i):
        return (i // (sizes[1] * sizes[2]), i // sizes[2] % sizes[1], i % sizes[2])

    mine, theirs = split(here), split(owner)
    slot = []
    for axis in range(3):
        n = sizes[axis]
        turn = jnp.where((mine[axis] + core) % 2 == 0, 1, -1)
        offset = (turn * (theirs[axis] - mine[axis]) + n) % n
        slot.append(sum(jnp.where(offset == e, i, 0) for i, e in enumerate(ARRIVAL[n])))
    place = jnp.zeros_like(block)
    for first, count, axes in PARTS:
        a, b, c = axes
        at = ((slot[c] * sizes[b] + slot[b]) * sizes[a] + slot[a]) * count + local - first
        place = jnp.where((local >= first) & (local < first + count), first * n_rows + at, place)
    return place


def pack_kernel(width, core_ref, tiles_ref, own_ref, send_ref):
    side = tiles_ref.shape[2]
    half = side // 2

    def fill(first, second):
        for q in range(tiles_ref.shape[1] // width):
            group = [tiles_ref[0, q * width + i] for i in range(width)]
            first[0, q] = jnp.concatenate([t[:, :half] for t in group], 1)
            second[0, q] = jnp.concatenate([t[:, half:] for t in group], 1)

    @pl.when(core_ref[0] == 0)
    def _():
        fill(own_ref, send_ref)

    @pl.when(core_ref[0] != 0)
    def _():
        fill(send_ref, own_ref)


def pack(core, tiles, width):
    rows, slots, side, _ = tiles.shape
    packed = jax.ShapeDtypeStruct((rows, slots // width, side, width * side // 2), BF)
    spec = pl.BlockSpec((1, slots // width, side, width * side // 2), lambda b: (b, 0, 0, 0))
    return pl.pallas_call(
        functools.partial(pack_kernel, width),
        grid=(rows,),
        in_specs=[
            pl.BlockSpec(memory_space=pltpu.SMEM),
            pl.BlockSpec((1, slots, side, side), lambda b: (b, 0, 0, 0)),
        ],
        out_specs=[
            spec,
            spec,
        ],
        out_shape=[packed, packed],
        compiler_params=pltpu.CompilerParams(vmem_limit_bytes=40 * 2**20),
        cost_estimate=pl.CostEstimate(flops=0, bytes_accessed=2**24, transcendentals=0),
        name="pack_tiles",
    )(core, tiles)


def forward_kernel(place_ref, own_ref, other_ref, *refs):
    *pieces, sum_ref, held, sems = refs
    b = pl.program_id(0)
    half = held.shape[1]

    @pl.when(b == 0)
    def _():
        copies = []
        low = 0
        for i, piece in enumerate(pieces):
            size = piece.shape[0]
            copies.append(pltpu.make_async_copy(piece, held.at[pl.ds(low, size)], sems.at[i]))
            low += size
        for copy in copies:
            copy.start()
        for copy in copies:
            copy.wait()

    total = jnp.zeros(sum_ref.shape[1:], F32)
    width = own_ref.shape[3] // half
    k = b * (place_ref.shape[0] // pl.num_programs(0))
    for ref in (own_ref, other_ref):
        for q in range(ref.shape[1]):
            right = jnp.concatenate([held[place_ref[k + i]] for i in range(width)], 0)
            total += jnp.dot(ref[0, q], right, preferred_element_type=F32)
            k += width
    sum_ref[0] = total


def forward(place, own, other, pieces):
    rows, groups, side, wide = own.shape
    n_tiles = sum(p.shape[0] for p in pieces)
    half, width = pieces[0].shape[1:]
    spec = pl.BlockSpec((1, groups, side, wide), lambda b: (b, 0, 0, 0))
    return pl.pallas_call(
        forward_kernel,
        grid=(rows,),
        in_specs=[pl.BlockSpec(memory_space=pltpu.SMEM), spec, spec]
        + [pl.BlockSpec(memory_space=pl.ANY)] * len(pieces),
        out_specs=pl.BlockSpec((1, side, width), lambda b: (b, 0, 0)),
        out_shape=jax.ShapeDtypeStruct((rows, side, width), F32),
        scratch_shapes=[
            pltpu.VMEM((n_tiles, half, width), BF),
            pltpu.SemaphoreType.DMA((len(pieces),)),
        ],
        compiler_params=pltpu.CompilerParams(vmem_limit_bytes=58 * 2**20),
        cost_estimate=pl.CostEstimate(flops=2**30, bytes_accessed=3 * 2**23, transcendentals=0),
        name="forward_tiles",
    )(place, own, other, *pieces)


def backward_kernel(
    core_ref, place_ref, mine_ref, came_ref, weight_ref, cot_ref, own_ref, other_ref, *refs
):
    act_ref, wgrad_ref, *terms, held, sems = refs
    b = pl.program_id(0)
    rows = pl.num_programs(0)
    half = held.shape[1]

    @pl.when(b == 0)
    def _():
        @pl.loop(0, held.shape[0] // 8)
        def _(i):
            held[pl.ds(i * 8, 8)] = jnp.zeros((8,) + held.shape[1:], BF)

    agg = (mine_ref[0] + came_ref[0]).astype(BF)
    weight = weight_ref[...]
    pre = jnp.dot(agg, weight, preferred_element_type=F32)
    sig = jax.nn.sigmoid(pre)
    act_ref[0] = (pre * sig).astype(BF)
    grad = (cot_ref[0].astype(F32) * sig * (1.0 + pre * (1.0 - sig))).astype(BF)
    spread = lax.dot_general(
        grad, weight, (((1,), (1,)), ((), ())), preferred_element_type=F32
    ).astype(BF)
    hid = grad.shape[1] // 2
    part = jnp.where(core_ref[0] == 0, grad[:, :hid].astype(F32), grad[:, hid:].astype(F32)).astype(BF)
    wgrad = lax.dot_general(agg, part, (((0,), (0,)), ((), ())), preferred_element_type=F32)

    @pl.when(b == 0)
    def _():
        wgrad_ref[...] = wgrad

    @pl.when(b > 0)
    def _():
        wgrad_ref[...] += wgrad

    width = own_ref.shape[3] // half
    k = b * (place_ref.shape[0] // rows)
    for ref in (own_ref, other_ref):
        for q in range(ref.shape[1]):
            term = lax.dot_general(
                ref[0, q], spread, (((0,), (0,)), ((), ())), preferred_element_type=F32
            ).astype(BF)
            for i in range(width):
                held[place_ref[k + i]] = term[i * half : (i + 1) * half]
            k += width

    @pl.when(b == rows - 1)
    def _():
        copies = []
        low = 0
        for i, out in enumerate(terms):
            size = out.shape[0]
            copies.append(pltpu.make_async_copy(held.at[pl.ds(low, size)], out, sems.at[i]))
            low += size
        for copy in copies:
            copy.start()
        for copy in copies:
            copy.wait()


def backward(core, place, mine, came, weight, cotangent, own, other, counts):
    rows, groups, side, wide = own.shape
    feat, hid = weight.shape
    tile_spec = pl.BlockSpec((1, groups, side, wide), lambda b: (b, 0, 0, 0))
    row_spec = pl.BlockSpec((1, side, feat), lambda b: (b, 0, 0))
    hid_spec = pl.BlockSpec((1, side, hid), lambda b: (b, 0, 0))
    smem = pl.BlockSpec(memory_space=pltpu.SMEM)
    return pl.pallas_call(
        backward_kernel,
        grid=(rows,),
        in_specs=[
            smem,
            smem,
            row_spec,
            row_spec,
            pl.BlockSpec((feat, hid), lambda b: (0, 0)),
            hid_spec,
            tile_spec,
            tile_spec,
        ],
        out_specs=[
            hid_spec,
            pl.BlockSpec((feat, hid // 2), lambda b: (0, 0)),
        ]
        + [pl.BlockSpec(memory_space=pl.ANY)] * len(counts),
        out_shape=[
            jax.ShapeDtypeStruct((rows, side, hid), BF),
            jax.ShapeDtypeStruct((feat, hid // 2), F32),
        ]
        + [jax.ShapeDtypeStruct((n, side // 2, feat), BF) for n in counts],
        scratch_shapes=[
            pltpu.VMEM((sum(counts), side // 2, feat), BF),
            pltpu.SemaphoreType.DMA((len(counts),)),
        ],
        compiler_params=pltpu.CompilerParams(vmem_limit_bytes=40 * 2**20),
        cost_estimate=pl.CostEstimate(flops=2**30, bytes_accessed=2**24, transcendentals=2**18),
        name="backward_tiles",
    )(core, place, mine, came, weight, cotangent, own, other)


def body(features, weight, tiles, tile_cols, order, cotangent):
    tile_rows, row_slots, side, _ = tiles.shape
    width = features.shape[1]
    n_tiles = order.shape[0]
    n_rows = lax.axis_size("rows")
    here = lax.axis_index("rows")
    core = lax.axis_index("rep")
    core_ref = core.reshape(1).astype(jnp.int32)
    half = side // 2
    group = 4 if row_slots % 4 == 0 else 2

    halves = features.reshape(tile_rows, 2, half, width)
    own_half = jnp.where(core == 0, halves[:, 0], halves[:, 1])
    labels = jnp.arange(n_tiles, dtype=jnp.int32)
    flat = tile_cols.reshape(-1)
    block = jnp.sum(jnp.where(flat[:, None] == labels[None, :], order[None, :], 0), axis=1)
    block = block.reshape(tile_rows, row_slots)
    first = late_sizes(n_rows)

    rounds = (((0, 1), (0, 1)),) * 4 + (
        ((0, 1), (0, 1)),
        ((0, 1, 2), (1, 2)),
        ((0, 1, 3), (0, 3)),
        ((0, 3), (0, 1, 3)),
        ((0, 1, 3), (0, 1, 3)),
    )
    single, pair = PARTS[0], PARTS[1:]
    chains = [
        gather_chain(n_rows, own_half[: single[1]], single[2]),
        gather_pair(n_rows, own_half[single[1] :], pair),
        index_chain(block),
        tile_chain(core_ref, tiles, group),
    ]
    pieces, pieces_pair, block, (own, other) = drive(chains, rounds if n_rows == 128 else ())
    pieces = pieces + pieces_pair[0] + pieces_pair[1]
    place = positions(n_rows, tile_rows, block, here, core)

    mine = forward(place, own, other, pieces)
    came = lax.ppermute(mine, "rep", SWAP)
    activated, wgrad, early, *late = backward(
        core_ref, arranged(n_rows, place, first), mine, came, weight,
        cotangent.reshape(tile_rows, side, -1), own, other, (n_tiles - sum(first),) + first,
    )

    every = (0, 1, 2)
    rounds = (
        (every, (0,)),
        ((0,), every),
        (every, every),
        (every, (1, 2)),
        ((1, 2), every),
    )
    buffers = []
    base = 0
    for (_, count, axes), out in zip(PARTS, late):
        size = count * n_rows - out.shape[0]
        buffers.append((early[base : base + size], out))
        base += size
    chains = [
        scatter_chain(n_rows, *buffers[0], single[2]),
        scatter_pair(n_rows, buffers[1:], pair),
        sum_chain(n_rows, wgrad),
    ]
    *owned, wgrad = drive(chains, rounds if n_rows == 128 else ())
    owned, wgrad = lax.optimization_barrier((jnp.concatenate(owned, 0), wgrad))
    wother = lax.ppermute(wgrad, "rep", SWAP)
    weight_grad = jnp.where(
        core == 0, jnp.concatenate([wgrad, wother], 1), jnp.concatenate([wother, wgrad], 1)
    )
    across = lax.ppermute(owned, "rep", SWAP)
    feature_grad = jnp.where(
        core == 0, jnp.stack([owned, across], 1), jnp.stack([across, owned], 1)
    ).reshape(tile_rows * side, width)
    return activated.reshape(tile_rows * side, -1), feature_grad, weight_grad


def solution(mesh):
    in_specs = (
        P("rows", None),
        P(),
        P("rows", "rep", None, None),
        P("rows", "rep"),
        P(),
        P("rows", None),
    )
    out_specs = (P("rows", None), P("rows", None), P())
    return jax.shard_map(body, mesh=mesh, in_specs=in_specs, out_specs=out_specs, check_vma=False)
```
